32 devices in a mesh: dp: 8 (over z, y), tensor: 4 (over x, core).
Axes of the slice: x: 2, y: 2, z: 4, core: 2. Of those that a mesh axis runs over, the one named last changes fastest.
Arguments:
- inputs: bfloat16 [12288, 1024], P('dp'), may hold values from -6 to 6
- cotangent: bfloat16 [12288, 1024], P('dp'), may hold values from -6 to 6
- lengths: int32 [24], P('dp'), may hold values from 50 to 500
- first_gain: float32 [1024], replicated, may hold values from 0.5 to 1.5
- first_bias: float32 [1024], replicated, may hold values from -1.5 to 1.5
- qkv_weight: bfloat16 [3, 1024, 1024], P(None, None, 'tensor'), may hold values from -0.1875 to 0.1875
- out_weight: bfloat16 [1024, 1024], P('tensor'), may hold values from -1.5 to 1.5
- first_scale: float32 [1024], replicated, may hold values from 0.5 to 1.5
- second_gain: float32 [1024], replicated, may hold values from 0.5 to 1.5
- second_bias: float32 [1024], replicated, may hold values from -1.5 to 1.5
- in_weight: bfloat16 [2, 1024, 4096], P(None, None, 'tensor'), may hold values from -0.1875 to 0.1875
- down_weight: bfloat16 [4096, 1024], P('tensor'), may hold values from -0.09375 to 0.09375
- second_scale: float32 [1024], replicated, may hold values from 0.5 to 1.5
Outputs:
- output: bfloat16 [12288, 1024], P('dp')
- input_grad: bfloat16 [12288, 1024], P('dp')
- first_gain_grad: float32 [1024], P('dp')
- first_bias_grad: float32 [1024], P('dp')
- qkv_grad: float32 [3, 1024, 1024], P(None, 'dp', 'tensor')
- out_grad: float32 [1024, 1024], P('tensor', 'dp')
- first_scale_grad: float32 [1024], P('dp')
- second_gain_grad: float32 [1024], P('dp')
- second_bias_grad: float32 [1024], P('dp')
- in_grad: float32 [2, 1024, 4096], P(None, 'dp', 'tensor')
- down_grad: float32 [4096, 1024], P('tensor', 'dp')
- second_scale_grad: float32 [1024], P('dp')
The draws below stay inside these ranges and needn't reach their ends.
All inputs are finite; a program needn't handle non-finite values.
Results may differ from the reference program's by a relative error of at most 0.025.
Values may be sent and summed in bfloat16 or wider, within the bound.
No kernel may reach another device: no remote copies, remote signals or barrier semaphores. Data moves between devices by JAX's collectives and lax.ppermute only.
A program may use at most 128 MiB of HBM per device.

```python
import jax
import jax.numpy as jnp
from jax import lax

D = 1024
HEADS = 16
HEAD = 64
FF = 4096
WINDOW = 128
CLIP = 512
CLIPS = 24
TOKENS = 12288
N_TENSOR = 4


def plant(drawn, key, smallest, high):
    spot = [jax.random.randint(jax.random.fold_in(key, axis), (), 0, length) for axis, length in enumerate(drawn.shape)]
    longest = drawn.shape.index(max(drawn.shape))
    neighbour = spot[:longest] + [(spot[longest] + 1) % drawn.shape[longest]] + spot[longest + 1:]
    return drawn.at[tuple(spot)].set(smallest).at[tuple(neighbour)].set(high)


def steps_of(key, extent, pieces, least, top_value):
    factor_of = 1.0
    for axis_at, shards_of in pieces:
        draws = jax.random.uniform(jax.random.fold_in(jax.random.fold_in(key, 6), axis_at), (shards_of,), jnp.float32, least / len(pieces), top_value / len(pieces))
        factor_of = factor_of * jnp.repeat(jnp.exp(draws), extent[axis_at] // shards_of).reshape((-1,) + (1,) * (len(extent) - 1 - axis_at))
    return factor_of


def normal_values(own_key, extent, deviation, reach, split=(), held_as=jnp.bfloat16):
    drawn = deviation * jax.random.normal(own_key, extent, jnp.float32)
    if split:
        drawn = drawn * steps_of(own_key, extent, split, -0.22, 0.18)
    return jnp.clip(drawn, -reach, reach).astype(held_as)


def setup_inputs(seed: int = 0) -> dict:
    arg_keys = jax.random.split(jax.random.key(seed), 14)
    inputs = normal_values(arg_keys[0], (TOKENS, D), 1.0, 6.0, ((0, 8),))
    cotangent = normal_values(arg_keys[1], (TOKENS, D), 1.0, 6.0, ((0, 8),))
    lengths = plant(jax.random.randint(arg_keys[2], (CLIPS,), CLIP * 50 // 512, CLIP - 11), jax.random.fold_in(arg_keys[2], 1), CLIP * 50 // 512, (CLIP - 11) - 1).astype(jnp.int32)
    first_gain = jnp.clip(1.0 + 0.1 * jax.random.normal(arg_keys[3], (D,), jnp.float32), 0.5, 1.5)
    first_bias = normal_values(arg_keys[4], (D,), 0.3, 1.5, (), jnp.float32)
    qkv_weight = normal_values(arg_keys[5], (3, D, D), D ** -0.5, 0.1875, ((2, 4),))
    out_weight = normal_values(arg_keys[6], (D, D), (D // 64) ** -0.5, 1.5, ((0, 4),))
    first_scale = jnp.clip(jax.random.uniform(arg_keys[7], (D,), jnp.float32, 0.5, 1.5), 0.5, 1.5)
    second_gain = jnp.clip(1.0 + 0.1 * jax.random.normal(arg_keys[8], (D,), jnp.float32), 0.5, 1.5)
    second_bias = normal_values(arg_keys[9], (D,), 0.3, 1.5, (), jnp.float32)
    in_weight = normal_values(arg_keys[10], (2, D, FF), D ** -0.5, 0.1875, ((2, 4),))
    down_weight = normal_values(arg_keys[11], (FF, D), FF ** -0.5, 0.09375, ((0, 4),))
    second_scale = jnp.clip(jax.random.uniform(arg_keys[12], (D,), jnp.float32, 0.5, 1.5), 0.5, 1.5)
    return dict(inputs=inputs, cotangent=cotangent, lengths=lengths, first_gain=first_gain, first_bias=first_bias, qkv_weight=qkv_weight, out_weight=out_weight, first_scale=first_scale, second_gain=second_gain, second_bias=second_bias, in_weight=in_weight, down_weight=down_weight, second_scale=second_scale)


@jax.custom_vjp
def low(v):
    return lax.optimization_barrier(v.astype(jnp.bfloat16)).astype(jnp.float32)

@jax.custom_vjp
def low_back(v):
    return v

def low_keep(v):
    return (low(v), None)

def low_pass(kept, grad):
    return (grad,)

def back_keep(v):
    return (v, None)

def back_low(kept, grad):
    return (low(grad),)
low.defvjp(low_keep, low_pass)
low_back.defvjp(back_keep, back_low)

def layer_norm(values, gain, bias):
    center = lax.optimization_barrier(jnp.mean(values, axis=-1, keepdims=True))
    shifted = values - center
    spread = lax.optimization_barrier(jnp.mean(shifted * shifted, axis=-1, keepdims=True))
    return shifted * lax.rsqrt(spread + 1e-05) * gain + bias

def rotary_tables():
    half_size = HEAD // 2
    frequency = 10000.0 ** (-2.0 * jnp.arange(half_size, dtype=jnp.float32) / HEAD)
    angles = jnp.arange(CLIP, dtype=jnp.float32)[:, None] * frequency[None, :]
    return (jnp.cos(angles)[:, None, :], jnp.sin(angles)[:, None, :])

def rotate(values, cosine, sine_table):
    half_size = HEAD // 2
    first_half = values[..., :half_size]
    second_half = values[..., half_size:]
    return jnp.concatenate([first_half * cosine - second_half * sine_table, second_half * cosine + first_half * sine_table], axis=-1)

def attend_clip(blocks):
    queries, key_rows, values, length = blocks
    scores = low_back(jnp.einsum('qhd,khd->hqk', queries, key_rows, precision=lax.Precision.HIGHEST) * HEAD ** (-0.5))
    position = jnp.arange(CLIP)
    allowed = (position[None, :] < length) & (jnp.abs(position[:, None] - position[None, :]) < WINDOW)
    scores = jnp.where(allowed[None], scores, -1e+30)
    maximum = lax.optimization_barrier(jnp.max(scores, axis=-1, keepdims=True))
    weights = jnp.exp(scores - maximum)
    probs_low = low(weights / lax.optimization_barrier(jnp.sum(weights, axis=-1, keepdims=True)))
    return jnp.einsum('hqk,khd->qhd', probs_low, values, precision=lax.Precision.HIGHEST)

def layer_forward(inputs, first_gain, first_bias, qkv_weight, out_weight, first_scale, second_gain, second_bias, in_weight, down_weight, second_scale, lengths):
    row_count = inputs.shape[0]
    clip_count = row_count // CLIP
    group_heads = HEADS // N_TENSOR
    group_width = group_heads * HEAD
    group_units = FF // N_TENSOR
    valid_rows = (jnp.arange(CLIP)[None, :] < lengths[:, None]).astype(jnp.float32).reshape(row_count, 1)
    cosine, sine_table = rotary_tables()
    normed_one = low(layer_norm(inputs, first_gain, first_bias))
    attention = jnp.zeros_like(inputs)
    for section in range(N_TENSOR):
        columns = slice(section * group_width, (section + 1) * group_width)
        shared_normed = low_back(normed_one)

        def project(index_c):
            return jnp.dot(shared_normed, qkv_weight[index_c][:, columns], precision=lax.Precision.HIGHEST).reshape(clip_count, CLIP, group_heads, HEAD)
        queries = low(rotate(low_back(project(0)), cosine, sine_table))
        key_rows = low(rotate(low_back(project(1)), cosine, sine_table))
        values = low(low_back(project(2)))
        head_out = lax.map(jax.checkpoint(attend_clip), (queries, key_rows, values, lengths))
        head_out = low(low_back(head_out)).reshape(row_count, group_width)
        attention = attention + low(jnp.dot(head_out, out_weight[columns, :], precision=lax.Precision.HIGHEST))
    attention = low_back(attention)
    hidden_one = inputs + first_scale * attention
    normed_two = low(layer_norm(hidden_one, second_gain, second_bias))
    feedforward = jnp.zeros_like(inputs)
    for section in range(N_TENSOR):
        unit_slice = slice(section * group_units, (section + 1) * group_units)
        shared_normed = low_back(normed_two)
        gate_pre = low_back(jnp.dot(shared_normed, in_weight[0][:, unit_slice], precision=lax.Precision.HIGHEST))
        up_pre = low_back(jnp.dot(shared_normed, in_weight[1][:, unit_slice], precision=lax.Precision.HIGHEST))
        activated = low(jax.nn.silu(gate_pre) * up_pre)
        feedforward = feedforward + low(jnp.dot(activated, down_weight[unit_slice, :], precision=lax.Precision.HIGHEST))
    feedforward = low_back(feedforward)
    return (hidden_one + second_scale * feedforward) * valid_rows

def reference(inputs, cotangent, lengths, first_gain, first_bias, qkv_weight, out_weight, first_scale, second_gain, second_bias, in_weight, down_weight, second_scale):
    arguments = (inputs, first_gain, first_bias, qkv_weight, out_weight, first_scale, second_gain, second_bias, in_weight, down_weight, second_scale)
    float_args = jax.tree.map(lambda array: array.astype(jnp.float32), arguments)

    def forward(*params_list):
        return layer_forward(*params_list, lengths)
    result, pullback = jax.vjp(forward, *float_args)
    gradients = pullback(cotangent.astype(jnp.float32))
    return (result.astype(jnp.bfloat16), gradients[0].astype(jnp.bfloat16), gradients[1], gradients[2], gradients[3], gradients[4], gradients[5], gradients[6], gradients[7], gradients[8], gradients[9], gradients[10])
```

```python
import functools

import jax
import jax.numpy as jnp
import numpy as np
from jax import lax
from jax.experimental import pallas as pl
from jax.experimental.pallas import tpu as pltpu
from jax.sharding import PartitionSpec as P

HEAD = 64
WINDOW = 128
CLIP = 512
HALF = CLIP // 2
TILE = 128
SPAN = 3 * TILE
MIB = 1024 * 1024
F32 = jnp.float32
BF16 = jnp.bfloat16


def tables():
    half_size = HEAD // 2
    frequency = (10000.0 ** (-2.0 * np.arange(half_size, dtype=np.float32) / HEAD)).astype(np.float32)
    angles = np.arange(CLIP, dtype=np.float32)[:, None] * frequency[None, :]
    cosine = np.cos(angles).astype(np.float32)
    sine = np.sin(angles).astype(np.float32)
    return (
        np.concatenate([cosine, cosine] * 2, axis=1),
        np.concatenate([-sine, sine] * 2, axis=1),
    )


def mm(a, b):
    return lax.dot_general(a, b, (((1,), (0,)), ((), ())), preferred_element_type=F32)


def mm_t(a, b):
    return lax.dot_general(a, b, (((1,), (1,)), ((), ())), preferred_element_type=F32)


def t_mm(a, b):
    return lax.dot_general(a, b, (((0,), (0,)), ((), ())), preferred_element_type=F32)


def normalize(values):
    center = jnp.mean(values, axis=-1, keepdims=True)
    shifted = values - center
    spread = jnp.mean(shifted * shifted, axis=-1, keepdims=True)
    inverse = lax.rsqrt(spread + 1e-05)
    return shifted * inverse, inverse


def norm_back(grad_normed, scaled, inverse, gain):
    weighted = grad_normed * gain
    centered = weighted - jnp.mean(weighted, axis=-1, keepdims=True)
    return inverse * (centered - scaled * jnp.mean(weighted * scaled, axis=-1, keepdims=True))


def swap_halves(values):
    width = values.shape[1]
    lane = lax.broadcasted_iota(jnp.int32, values.shape, 1)
    up = pltpu.roll(values, width - HEAD // 2, 1)
    down = pltpu.roll(values, HEAD // 2, 1)
    return jnp.where(lane % HEAD < HEAD // 2, up, down)


def wide(table, width):
    return jnp.concatenate([table] * (width // table.shape[1]), axis=1)


def lane_masks(width, dtype):
    lane = lax.broadcasted_iota(jnp.int32, (1, width), 1) // HEAD
    return [(lane == head).astype(F32).astype(dtype) for head in range(width // HEAD)]


def stack_heads(rows, masks):
    return jnp.concatenate([rows * mask for mask in masks], axis=0)


def pick_heads(stacked, masks):
    total = stacked[:TILE] * masks[0]
    for head in range(1, len(masks)):
        total = total + stacked[head * TILE : (head + 1) * TILE] * masks[head]
    return total


def probabilities(queries, keys, tile, length, heads):
    scores = mm_t(queries, keys)
    row = lax.broadcasted_iota(jnp.int32, scores.shape, 0) % TILE
    column = lax.broadcasted_iota(jnp.int32, scores.shape, 1)
    ahead = column - row
    key = column + (tile - 1) * TILE
    allowed = (ahead > 0) & (ahead < 2 * WINDOW) & (key >= 0) & (key < length)
    scores = jnp.where(allowed, scores, -1e30)
    maximum = jnp.max(scores, axis=-1, keepdims=True)
    weights = jnp.exp(scores - maximum)
    return weights * (1.0 / jnp.sum(weights, axis=-1, keepdims=True))


def attend_kernel(
    clip, meta, x_ref, gain, bias, w_qkv, w_out, cos_ref, sin_ref,
    normed, q_out, k_out, v_out, heads_out, keep, send, k_pad, v_pad,
):
    core = meta[0]
    length = meta[1 + clip]
    width = w_out.shape[0]
    edge = jnp.zeros((TILE, width), BF16)
    for pad in (k_pad, v_pad):
        pad[:TILE] = edge
        pad[TILE + CLIP :] = edge
    value_sum = jnp.zeros((1, width), F32)
    for half in range(2):
        rows = slice(half * HALF, (half + 1) * HALF)
        scaled, _ = normalize(x_ref[rows].astype(F32))
        low = (scaled * gain[...] + bias[...]).astype(BF16)
        normed[rows] = low
        cosine = wide(cos_ref[rows], width)
        sine = wide(sin_ref[rows], width)
        queries = mm(low, w_qkv[0])
        q_out[rows] = (queries * cosine + swap_halves(queries) * sine).astype(BF16)
        keys = mm(low, w_qkv[1])
        keys = (keys * cosine + swap_halves(keys) * sine).astype(BF16)
        k_out[rows] = keys
        k_pad[pl.ds(TILE + half * HALF, HALF)] = keys
        values = mm(low, w_qkv[2]).astype(BF16)
        v_out[rows] = values
        v_pad[pl.ds(TILE + half * HALF, HALF)] = values
        value_sum = value_sum + jnp.sum(values.astype(F32), axis=0, keepdims=True)
    low_masks = lane_masks(width, BF16)
    masks = lane_masks(width, F32)
    scale = jnp.asarray(HEAD ** -0.5, BF16)
    for tile in range(CLIP // TILE):
        rows = slice(tile * TILE, (tile + 1) * TILE)
        window = slice(tile * TILE, tile * TILE + SPAN)
        stacked = stack_heads(q_out[rows] * scale, low_masks)
        probs = probabilities(stacked, k_pad[window], tile, length, len(masks)).astype(BF16)
        mixed = pick_heads(mm(probs, v_pad[window]), masks)
        position = lax.broadcasted_iota(jnp.int32, mixed.shape, 0) + tile * TILE
        mixed = jnp.where(position >= length + WINDOW - 1, value_sum * (1.0 / CLIP), mixed)
        heads_out[rows] = mixed.astype(BF16)
    for target, part in ((send, 1 - core), (keep, core)):
        rows = pl.ds(pl.multiple_of(part * HALF, HALF), HALF)
        target[...] = mm(heads_out[rows], w_out[...]).astype(BF16)


def attend_back_kernel(
    clip, meta, ga_own, ga_other, w_out, q_ref, k_ref, v_ref, w_qkv, cos_ref, sin_ref, x_ref,
    grads, keep, send, sums, k_pad, v_pad, dk, dv, gh, dq,
):
    core = meta[0]
    length = meta[1 + clip]
    width = w_out.shape[0]
    edge = jnp.zeros((TILE, width), BF16)
    for pad, source in ((k_pad, k_ref), (v_pad, v_ref)):
        pad[:TILE] = edge
        pad[TILE + CLIP :] = edge
        pad[TILE : TILE + CLIP] = source[...]
    dk[...] = jnp.zeros_like(dk)
    dv[...] = jnp.zeros_like(dv)
    for source, part in ((ga_own, core), (ga_other, 1 - core)):
        rows = pl.ds(pl.multiple_of(part * HALF, HALF), HALF)
        gh[rows] = mm_t(source[...], w_out[...]).astype(BF16)
    low_masks = lane_masks(width, BF16)
    masks = lane_masks(width, F32)
    scale = jnp.asarray(HEAD ** -0.5, BF16)
    for tile in range(CLIP // TILE):
        rows = slice(tile * TILE, (tile + 1) * TILE)
        window = slice(tile * TILE, tile * TILE + SPAN)
        stacked = stack_heads(q_ref[rows] * scale, low_masks)
        grad_out = stack_heads(gh[rows], low_masks)
        probs = probabilities(stacked, k_pad[window], tile, length, len(masks))
        grad_probs = mm_t(grad_out, v_pad[window])
        inner = jnp.sum(probs * grad_probs, axis=-1, keepdims=True)
        grad_scores = (probs * (grad_probs - inner)).astype(BF16)
        dq[rows] = pick_heads(mm(grad_scores, k_pad[window]), masks) * HEAD ** -0.5
        dk[window] += t_mm(grad_scores, stacked)
        dv[window] += t_mm(probs.astype(BF16), grad_out)
    cosine = wide(cos_ref[...], width)
    sine = wide(sin_ref[...], width)
    inside = slice(TILE, TILE + CLIP)
    grad = dq[...]
    grads[:, :width] = (grad * cosine - swap_halves(grad) * sine).astype(BF16)
    grad = dk[inside]
    grads[:, width : 2 * width] = (grad * cosine - swap_halves(grad) * sine).astype(BF16)
    grads[:, 2 * width :] = dv[inside].astype(BF16)
    sums[...] = jnp.zeros_like(sums)
    for target, part in ((send, 1 - core), (keep, core)):
        rows = pl.ds(pl.multiple_of(part * HALF, HALF), HALF)
        term = mm_t(grads[rows, :width], w_qkv[0])
        term = term + mm_t(grads[rows, width : 2 * width], w_qkv[1])
        term = term + mm_t(grads[rows, 2 * width :], w_qkv[2])
        low = term.astype(BF16)
        target[...] = low
        term = low.astype(F32)
        scaled, _ = normalize(x_ref[rows].astype(F32))
        sums[0:1] += jnp.sum(term * scaled, axis=0, keepdims=True)
        sums[1:2] += jnp.sum(term, axis=0, keepdims=True)


def feed_kernel(
    clip, meta, n_own, n_other, cot, scale_two, w_in, w_down,
    act_out, gate_out, up_out, gf_out, ff_keep, ff_send, gn_keep, gn_send,
    rows_in, ff_acc, gn_acc,
):
    step = pl.program_id(0)
    core = meta[0]
    length = meta[1 + clip]

    @pl.when(step == 0)
    def _():
        rows_in[:HALF] = n_own[...]
        rows_in[HALF:] = n_other[...]
        for place, part in ((0, core), (1, 1 - core)):
            rows = pl.ds(pl.multiple_of(part * HALF, HALF), HALF)
            grad = cot[rows].astype(F32)
            position = lax.broadcasted_iota(jnp.int32, grad.shape, 0) + part * HALF
            grad = jnp.where(position < length, grad, 0.0) * scale_two[...]
            gf_out[place * HALF : (place + 1) * HALF] = grad.astype(BF16)
        ff_acc[...] = jnp.zeros_like(ff_acc)
        gn_acc[...] = jnp.zeros_like(gn_acc)

    for part in range(2):
        rows = slice(part * HALF, (part + 1) * HALF)
        low = rows_in[rows]
        gate = mm(low, w_in[0])
        up = mm(low, w_in[1])
        grad_act = mm_t(gf_out[rows], w_down[...])
        sg = 1.0 / (1.0 + jnp.exp(-gate))
        silu = gate * sg
        act = (silu * up).astype(BF16)
        grad_gate = (grad_act * up * (sg + silu * (1.0 - sg))).astype(BF16)
        grad_up = (grad_act * silu).astype(BF16)
        act_out[rows] = act
        gate_out[rows] = grad_gate
        up_out[rows] = grad_up
        ff_acc[rows] += mm(act, w_down[...])
        gn_acc[rows] += mm_t(grad_gate, w_in[0]) + mm_t(grad_up, w_in[1])

    @pl.when(step == pl.num_programs(0) - 1)
    def _():
        ff_keep[...] = ff_acc[:HALF].astype(BF16)
        ff_send[...] = ff_acc[HALF:].astype(BF16)
        gn_keep[...] = gn_acc[:HALF].astype(BF16)
        gn_send[...] = gn_acc[HALF:].astype(BF16)


def middle_kernel(meta, own, other, x_ref, scale_one, gain, bias, out):
    attention = own[...].astype(F32) + other[...].astype(F32)
    hidden = x_ref[...].astype(F32) + scale_one[...] * attention
    scaled, _ = normalize(hidden)
    out[...] = (scaled * gain[...] + bias[...]).astype(BF16)


def valid_cot(clip, meta, cot, rows):
    position = lax.broadcasted_iota(jnp.int32, cot.shape, 0) + pl.program_id(0) * rows + meta[0] * HALF
    return jnp.where(position < meta[1 + clip], cot[...].astype(F32), 0.0), position


def middle_back_kernel(
    clip, meta, own, other, g_own, g_other, x_ref, cot, scale_one, gain, grad_out, low_out, sums
):
    attention = own[...].astype(F32) + other[...].astype(F32)
    hidden = x_ref[...].astype(F32) + scale_one[...] * attention
    scaled, inverse = normalize(hidden)
    grad_normed = g_own[...].astype(F32) + g_other[...].astype(F32)
    grad_two, _ = valid_cot(clip, meta, cot, x_ref.shape[0])
    grad_one = grad_two + norm_back(grad_normed, scaled, inverse, gain[...])
    grad_out[...] = grad_one
    low_out[...] = (grad_one * scale_one[...]).astype(BF16)

    @pl.when(pl.program_id(0) == 0)
    def _():
        sums[...] = jnp.zeros_like(sums)

    sums[0:1] += jnp.sum(grad_one * attention, axis=0, keepdims=True)
    sums[1:2] += jnp.sum(grad_normed * scaled, axis=0, keepdims=True)
    sums[2:3] += jnp.sum(grad_normed, axis=0, keepdims=True)


def output_kernel(clip, meta, own, other, f_own, f_other, x_ref, cot, scale_one, scale_two, out, sums):
    attention = own[...].astype(F32) + other[...].astype(F32)
    hidden = x_ref[...].astype(F32) + scale_one[...] * attention
    forward = f_own[...].astype(F32) + f_other[...].astype(F32)
    grad_two, position = valid_cot(clip, meta, cot, x_ref.shape[0])
    result = hidden + scale_two[...] * forward
    out[...] = jnp.where(position < meta[1 + clip], result, 0.0).astype(BF16)

    @pl.when(pl.program_id(0) == 0)
    def _():
        sums[...] = jnp.zeros_like(sums)

    sums[0:1] += jnp.sum(grad_two * forward, axis=0, keepdims=True)


def input_back_kernel(meta, g_own, g_other, x_ref, grad_one, gain, out):
    scaled, inverse = normalize(x_ref[...].astype(F32))
    grad_normed = g_own[...].astype(F32) + g_other[...].astype(F32)
    out[...] = (grad_one[...] + norm_back(grad_normed, scaled, inverse, gain[...])).astype(BF16)


def weight_grad_kernel(left_count, *refs):
    left = refs[:left_count]
    right = refs[left_count:-2]
    out, turned = refs[-2:]

    @pl.when(pl.program_id(0) == 0)
    def _():
        start = 0
        for piece in left:
            turned[:, start : start + piece.shape[0]] = piece[...].T
            start += piece.shape[0]

    rhs = jnp.concatenate([piece[...] for piece in right], axis=0)
    out[...] = mm(turned[...], rhs).astype(BF16)


def params(limit, **kw):
    return pltpu.CompilerParams(vmem_limit_bytes=limit * MIB, **kw)


def shape(rows, columns, dtype=BF16):
    return jax.ShapeDtypeStruct((rows, columns), dtype)


def whole(*dims):
    return pl.BlockSpec(dims, lambda i, *_: (0,) * len(dims))


def smem():
    return pl.BlockSpec(memory_space=pltpu.SMEM)


def weight_grad(left, right, block=256):
    rows = sum(piece.shape[0] for piece in left)
    depth = left[0].shape[1]
    width = right[0].shape[1]
    return pl.pallas_call(
        functools.partial(weight_grad_kernel, len(left)),
        grid=(width // block,),
        in_specs=[whole(*piece.shape) for piece in left]
        + [pl.BlockSpec((piece.shape[0], block), lambda i: (0, i)) for piece in right],
        out_specs=pl.BlockSpec((depth, block), lambda i: (0, i)),
        out_shape=shape(depth, width),
        scratch_shapes=[pltpu.VMEM((depth, rows), BF16)],
        compiler_params=params(40),
        cost_estimate=pl.CostEstimate(
            flops=2 * rows * depth * width,
            bytes_accessed=2 * (rows * depth + rows * width + depth * width),
            transcendentals=0,
        ),
    )(*left, *right)


def build(dp_size):
    cos_np, sin_np = tables()

    def per_device(
        inputs, cotangent, lengths, first_gain, first_bias, qkv_weight, out_weight, first_scale,
        second_gain, second_bias, in_weight, down_weight, second_scale,
    ):
        clips = lengths.shape[0]
        depth = inputs.shape[1]
        width = out_weight.shape[0]
        units = down_weight.shape[0]
        place = lax.axis_index("tensor")
        core = place % 2
        meta = jnp.concatenate([core.reshape(1).astype(jnp.int32), lengths])
        cos_t = jnp.asarray(cos_np)
        sin_t = jnp.asarray(sin_np)
        row = lambda v: v.reshape(1, depth)
        first_gain, first_bias, first_scale = row(first_gain), row(first_bias), row(first_scale)
        second_gain, second_bias, second_scale = row(second_gain), row(second_bias), row(second_scale)

        def swap(values, bit):
            return lax.ppermute(values, "tensor", [(i, i ^ bit) for i in range(4)])

        def pair_sum(keep, send):
            arrived = swap(send, 1)
            return (keep.astype(F32) + arrived.astype(F32)).astype(BF16)

        def attend(clip):
            flops = 2 * CLIP * depth * 4 * width + 4 * 4 * CLIP * SPAN * width
            return pl.pallas_call(
                functools.partial(attend_kernel, clip),
                grid=(1,),
                in_specs=[
                    smem(), pl.BlockSpec((CLIP, depth), lambda i: (clip, 0)), whole(1, depth),
                    whole(1, depth), whole(3, depth, width), whole(width, depth),
                    whole(CLIP, 128), whole(CLIP, 128),
                ],
                out_specs=[whole(CLIP, depth)] + [whole(CLIP, width)] * 4 + [whole(HALF, depth)] * 2,
                out_shape=[shape(CLIP, depth)] + [shape(CLIP, width)] * 4 + [shape(HALF, depth)] * 2,
                scratch_shapes=[pltpu.VMEM((CLIP + 2 * TILE, width), BF16)] * 2,
                compiler_params=params(40),
                cost_estimate=pl.CostEstimate(
                    flops=flops, bytes_accessed=7 * MIB, transcendentals=4 * CLIP * SPAN
                ),
            )(meta, inputs, first_gain, first_bias, qkv_weight, out_weight, cos_t, sin_t)

        def attend_back(clip, own, other, q, k, v):
            flops = 2 * CLIP * depth * 4 * width + 10 * 4 * CLIP * SPAN * width
            pad = (CLIP + 2 * TILE, width)
            return pl.pallas_call(
                functools.partial(attend_back_kernel, clip),
                grid=(1,),
                in_specs=[
                    smem(), whole(HALF, depth), whole(HALF, depth), whole(width, depth),
                    whole(CLIP, width), whole(CLIP, width), whole(CLIP, width),
                    whole(3, depth, width), whole(CLIP, 128), whole(CLIP, 128),
                    pl.BlockSpec((CLIP, depth), lambda i: (clip, 0)),
                ],
                out_specs=[
                    whole(CLIP, 3 * width), whole(HALF, depth), whole(HALF, depth), whole(8, depth)
                ],
                out_shape=[
                    shape(CLIP, 3 * width), shape(HALF, depth), shape(HALF, depth),
                    shape(8, depth, F32),
                ],
                scratch_shapes=[
                    pltpu.VMEM(pad, BF16), pltpu.VMEM(pad, BF16), pltpu.VMEM(pad, F32),
                    pltpu.VMEM(pad, F32), pltpu.VMEM((CLIP, width), BF16),
                    pltpu.VMEM((CLIP, width), F32),
                ],
                compiler_params=params(40),
                cost_estimate=pl.CostEstimate(
                    flops=flops, bytes_accessed=8 * MIB, transcendentals=4 * CLIP * SPAN
                ),
            )(meta, own, other, out_weight, q, k, v, qkv_weight, cos_t, sin_t, inputs)

        def feed(clip, own, other):
            block = 256
            half = [shape(HALF, depth)] * 4
            return pl.pallas_call(
                functools.partial(feed_kernel, clip),
                grid=(units // block,),
                in_specs=[
                    smem(), whole(HALF, depth), whole(HALF, depth),
                    pl.BlockSpec((CLIP, depth), lambda i: (clip, 0)), whole(1, depth),
                    pl.BlockSpec((2, depth, block), lambda i: (0, 0, i)),
                    pl.BlockSpec((block, depth), lambda i: (i, 0)),
                ],
                out_specs=[pl.BlockSpec((CLIP, block), lambda i: (0, i))] * 3
                + [whole(CLIP, depth)] + [whole(HALF, depth)] * 4,
                out_shape=[shape(CLIP, units)] * 3 + [shape(CLIP, depth)] + half,
                scratch_shapes=[
                    pltpu.VMEM((CLIP, depth), BF16), pltpu.VMEM((CLIP, depth), F32),
                    pltpu.VMEM((CLIP, depth), F32),
                ],
                compiler_params=params(48),
                cost_estimate=pl.CostEstimate(
                    flops=12 * CLIP * depth * units, bytes_accessed=14 * MIB,
                    transcendentals=CLIP * units,
                ),
            )(meta, own, other, cotangent, second_scale, in_weight, down_weight)

        tile = 128
        steps = HALF // tile

        def rowwise(body, clip, local, full, shared, outs, sums):
            part = pl.BlockSpec((tile, depth), lambda i, m: (i, 0))
            spot = pl.BlockSpec((tile, depth), lambda i, m: ((2 * clip + m[0]) * steps + i, 0))
            out_shape = [shape(HALF, depth, dtype) for dtype in outs]
            out_specs = [part] * len(outs)
            if sums:
                out_shape.append(shape(8, depth, F32))
                out_specs.append(whole(8, depth))
            return pl.pallas_call(
                body,
                grid_spec=pltpu.PrefetchScalarGridSpec(
                    num_scalar_prefetch=1,
                    grid=(steps,),
                    in_specs=[part] * len(local) + [spot] * len(full) + [whole(1, depth)] * len(shared),
                    out_specs=out_specs,
                ),
                out_shape=out_shape,
                compiler_params=params(32),
                cost_estimate=pl.CostEstimate(
                    flops=20 * HALF * depth, bytes_accessed=3 * MIB, transcendentals=0
                ),
            )(meta, *local, *full, *shared)

        def middle(clip, own, other):
            return rowwise(
                middle_kernel, clip, [own, other], [inputs],
                [first_scale, second_gain, second_bias], [BF16], False,
            )[0]

        normed, q, k, v, heads, att_own, att_other = ([None] * clips for _ in range(7))
        n_own, n_other = [None] * clips, [None] * clips
        act, d_gate, d_up, gf, ff_own, gn_own = ([None] * clips for _ in range(6))
        for c in range(clips):
            normed[c], q[c], k[c], v[c], heads[c], keep, send = attend(c)
            att_own[c] = pair_sum(keep, send)
            att_other[c] = swap(att_own[c], 2)
        for c in range(clips):
            n_own[c] = middle(c, att_own[c], att_other[c])
            n_other[c] = swap(n_own[c], 1)
        for c in range(clips):
            act[c], d_gate[c], d_up[c], gf[c], ff_keep, ff_send, gn_keep, gn_send = feed(
                c, n_own[c], n_other[c]
            )
            gn_own[c] = pair_sum(gn_keep, gn_send)
            ff_own[c] = pair_sum(ff_keep, ff_send)
        left = [piece for c in range(clips) for piece in (n_own[c], n_other[c])]
        grad_in = [weight_grad(left, d_gate), weight_grad(left, d_up)]
        grad_down = weight_grad(gf, act)

        vectors = []
        ga_own, ga_other, grad_one, d_qkv, g1_own = ([None] * clips for _ in range(5))
        for c in range(clips):
            gn_other = swap(gn_own[c], 2)
            grad_one[c], ga_own[c], sums = rowwise(
                functools.partial(middle_back_kernel, c), c,
                [att_own[c], att_other[c], gn_own[c], gn_other], [inputs, cotangent],
                [first_scale, second_gain], [F32, BF16], True,
            )
            ga_other[c] = swap(ga_own[c], 1)
            vectors.append((sums[0:1], 2, sums[1:2], 3, sums[2:3], 4))
        back_sums = None
        for c in range(clips):
            d_qkv[c], keep, send, sums = attend_back(c, ga_own[c], ga_other[c], q[c], k[c], v[c])
            g1_own[c] = pair_sum(keep, send)
            back_sums = sums if back_sums is None else back_sums + sums

        def natural(own, other):
            pieces = []
            for a, b in zip(own, other):
                pieces += [jnp.where(core == 0, a, b), jnp.where(core == 0, b, a)]
            return jnp.concatenate(pieces, axis=0)

        out_own, out_other = [], []
        scale_sums = 0.0
        for c in range(clips):
            ff_other = swap(ff_own[c], 2)
            result, sums = rowwise(
                functools.partial(output_kernel, c), c,
                [att_own[c], att_other[c], ff_own[c], ff_other], [inputs, cotangent],
                [first_scale, second_scale], [BF16], True,
            )
            scale_sums = scale_sums + sums[0:1]
            out_own.append(result)
            out_other.append(swap(result, 1))
        output = natural(out_own, out_other)

        in_own, in_other = [], []
        for c in range(clips):
            g1_other = swap(g1_own[c], 2)
            result = rowwise(
                input_back_kernel, c, [g1_own[c], g1_other], [inputs], [], [BF16], False
            )[0] if False else pl.pallas_call(
                input_back_kernel,
                grid_spec=pltpu.PrefetchScalarGridSpec(
                    num_scalar_prefetch=1,
                    grid=(steps,),
                    in_specs=[
                        pl.BlockSpec((tile, depth), lambda i, m: (i, 0)),
                        pl.BlockSpec((tile, depth), lambda i, m: (i, 0)),
                        pl.BlockSpec((tile, depth), lambda i, m: ((2 * c + m[0]) * steps + i, 0)),
                        pl.BlockSpec((tile, depth), lambda i, m: (i, 0)),
                        whole(1, depth),
                    ],
                    out_specs=pl.BlockSpec((tile, depth), lambda i, m: (i, 0)),
                ),
                out_shape=shape(HALF, depth),
                compiler_params=params(32),
                cost_estimate=pl.CostEstimate(
                    flops=20 * HALF * depth, bytes_accessed=3 * MIB, transcendentals=0
                ),
            )(meta, g1_own[c], g1_other, inputs, grad_one[c], first_gain)
            in_own.append(result)
            in_other.append(swap(result, 1))
        input_grad = natural(in_own, in_other)

        left = normed
        grad_qkv = weight_grad(normed, d_qkv)
        heads_own = []
        for c in range(clips):
            for part in (core, 1 - core):
                heads_own.append(lax.dynamic_slice_in_dim(heads[c], part * HALF, HALF, 0))
        left = [piece for c in range(clips) for piece in (ga_own[c], ga_other[c])]
        grad_out = weight_grad(left, heads_own)

        middle_sums = sum(jnp.concatenate([a, b, d], axis=0) for a, _, b, _, d, _ in vectors)
        alike = jnp.concatenate([middle_sums, scale_sums], axis=0)
        alike = jnp.where(place < 2, alike, 0.0)
        stacked = jnp.concatenate(
            [back_sums[0:2], alike, jnp.zeros((2, depth), F32)], axis=0
        )
        for bit in (1, 2):
            stacked = stacked + swap(stacked, bit)
        bit = 1
        while bit < dp_size:
            stacked = stacked + lax.ppermute(
                stacked, "dp", [(i, i ^ bit) for i in range(dp_size)]
            )
            bit *= 2
        spot = lax.axis_index("dp")
        share = depth // dp_size
        mine = lax.dynamic_slice_in_dim(stacked, spot * share, share, 1)

        def scatter(grads):
            columns = grads.shape[1]
            if dp_size != 8:
                return lax.psum_scatter(grads, "dp", scatter_dimension=0, tiled=True).astype(F32)
            y = spot % 2
            z = spot // 2
            cut = grads.reshape(4, 2, share, columns)
            send = lax.dynamic_index_in_dim(cut, 1 - y, 1, False)
            keep = lax.dynamic_index_in_dim(cut, y, 1, False)
            arrived = lax.ppermute(send, "dp", [(i, i ^ 1) for i in range(8)])
            pair = (keep.astype(F32) + arrived.astype(F32)).astype(BF16)
            total = lax.dynamic_index_in_dim(pair, z, 0, False).astype(F32)
            for hop in (1, 2, 3):
                piece = lax.dynamic_index_in_dim(pair, z ^ hop, 0, False)
                piece = lax.ppermute(piece, "dp", [(i, i ^ (2 * hop)) for i in range(8)])
                total = total + piece.astype(F32)
            return total

        in_sum = [scatter(g) for g in grad_in]
        down_sum = scatter(grad_down)
        qkv_sum = scatter(grad_qkv)
        out_sum = scatter(grad_out)
        return (
            output,
            input_grad,
            mine[0],
            mine[1],
            jnp.stack([qkv_sum[:, i * width : (i + 1) * width] for i in range(3)]),
            out_sum.T,
            mine[2],
            mine[3],
            mine[4],
            jnp.stack(in_sum),
            down_sum.T,
            mine[5],
        )

    return per_device


def solution(mesh):
    placed = (
        P("dp", None), P("dp", None), P("dp"), P(), P(), P(None, None, "tensor"),
        P("tensor", None), P(), P(), P(), P(None, None, "tensor"), P("tensor", None), P(),
    )
    return jax.shard_map(
        build(mesh.shape["dp"]),
        mesh=mesh,
        in_specs=placed,
        out_specs=(
            P("dp", None), P("dp", None), P("dp"), P("dp"), P(None, "dp", "tensor"),
            P("tensor", "dp"), P("dp"), P("dp"), P("dp"), P(None, "dp", "tensor"),
            P("tensor", "dp"), P("dp"),
        ),
        check_vma=False,
    )
```

```python
import functools

import jax
import jax.numpy as jnp
import numpy as np
from jax import lax
from jax.experimental import pallas as pl
from jax.experimental.pallas import tpu as pltpu
from jax.sharding import PartitionSpec as P

HEAD = 64
WINDOW = 128
CLIP = 512
HALF = CLIP // 2
TILE = 128
SPAN = 3 * TILE
MIB = 1024 * 1024
F32 = jnp.float32
BF16 = jnp.bfloat16


def tables():
    half_size = HEAD // 2
    frequency = (10000.0 ** (-2.0 * np.arange(half_size, dtype=np.float32) / HEAD)).astype(np.float32)
    angles = np.arange(CLIP, dtype=np.float32)[:, None] * frequency[None, :]
    cosine = np.cos(angles).astype(np.float32)
    sine = np.sin(angles).astype(np.float32)
    return (
        np.concatenate([cosine, cosine] * 2, axis=1),
        np.concatenate([-sine, sine] * 2, axis=1),
    )


def mm(a, b):
    return lax.dot_general(a, b, (((1,), (0,)), ((), ())), preferred_element_type=F32)


def mm_t(a, b):
    return lax.dot_general(a, b, (((1,), (1,)), ((), ())), preferred_element_type=F32)


def t_mm(a, b):
    return lax.dot_general(a, b, (((0,), (0,)), ((), ())), preferred_element_type=F32)


def normalize(values):
    center = jnp.mean(values, axis=-1, keepdims=True)
    shifted = values - center
    spread = jnp.mean(shifted * shifted, axis=-1, keepdims=True)
    inverse = lax.rsqrt(spread + 1e-05)
    return shifted * inverse, inverse


def norm_back(grad_normed, scaled, inverse, gain):
    weighted = grad_normed * gain
    centered = weighted - jnp.mean(weighted, axis=-1, keepdims=True)
    return inverse * (centered - scaled * jnp.mean(weighted * scaled, axis=-1, keepdims=True))


def swap_halves(values):
    width = values.shape[1]
    lane = lax.broadcasted_iota(jnp.int32, values.shape, 1)
    up = pltpu.roll(values, width - HEAD // 2, 1)
    down = pltpu.roll(values, HEAD // 2, 1)
    return jnp.where(lane % HEAD < HEAD // 2, up, down)


def wide(table, width):
    return jnp.concatenate([table] * (width // table.shape[1]), axis=1)


def lane_masks(width, dtype):
    lane = lax.broadcasted_iota(jnp.int32, (1, width), 1) // HEAD
    return [(lane == head).astype(F32).astype(dtype) for head in range(width // HEAD)]


def stack_heads(rows, masks):
    return jnp.concatenate([rows * mask for mask in masks], axis=0)


def pick_heads(stacked, masks):
    total = stacked[:TILE] * masks[0]
    for head in range(1, len(masks)):
        total = total + stacked[head * TILE : (head + 1) * TILE] * masks[head]
    return total


def probabilities(queries, keys, tile, length):
    scores = mm_t(queries, keys)
    row = lax.broadcasted_iota(jnp.int32, scores.shape, 0) % TILE
    column = lax.broadcasted_iota(jnp.int32, scores.shape, 1)
    ahead = column - row
    key = column + (tile - 1) * TILE
    allowed = (ahead > 0) & (ahead < 2 * WINDOW) & (key >= 0) & (key < length)
    scores = jnp.where(allowed, scores, -1e30)
    maximum = jnp.max(scores, axis=-1, keepdims=True)
    weights = jnp.exp(scores - maximum)
    return weights * (1.0 / jnp.sum(weights, axis=-1, keepdims=True))


def attend_kernel(
    first, meta, x_ref, gain, bias, w_qkv, cos_ref, sin_ref,
    normed, q_out, k_out, v_out, heads_out, send, q_all, k_pad, v_pad, value_sum,
):
    step = pl.program_id(0)
    half = step % 2
    core = meta[0]
    length = meta[1 + first + step // 2]
    width = w_qkv.shape[2]

    @pl.when(step == 0)
    def _():
        edge = jnp.zeros((TILE, width), BF16)
        for pad in (k_pad, v_pad):
            pad[:TILE] = edge
            pad[TILE + CLIP :] = edge

    scaled, _ = normalize(x_ref[...].astype(F32))
    low = (scaled * gain[...] + bias[...]).astype(BF16)
    normed[...] = low
    rows = pl.ds(pl.multiple_of(half * HALF, HALF), HALF)
    inside = pl.ds(pl.multiple_of(half * HALF + TILE, TILE), HALF)
    cosine = wide(cos_ref[rows], width)
    sine = wide(sin_ref[rows], width)
    queries = mm(low, w_qkv[0])
    queries = (queries * cosine + swap_halves(queries) * sine).astype(BF16)
    q_out[...] = queries
    q_all[rows] = queries
    keys = mm(low, w_qkv[1])
    keys = (keys * cosine + swap_halves(keys) * sine).astype(BF16)
    k_out[...] = keys
    k_pad[inside] = keys
    values = mm(low, w_qkv[2]).astype(BF16)
    v_out[...] = values
    v_pad[inside] = values
    total = jnp.sum(values.astype(F32), axis=0, keepdims=True)
    value_sum[...] = jnp.where(half == 0, total, value_sum[...] + total)

    @pl.when(half == 1)
    def _():
        low_masks = lane_masks(width, BF16)
        masks = lane_masks(width, F32)
        scale = jnp.asarray(HEAD ** -0.5, BF16)
        for tile in range(CLIP // TILE):
            rows = slice(tile * TILE, (tile + 1) * TILE)
            window = slice(tile * TILE, tile * TILE + SPAN)
            stacked = stack_heads(q_all[rows] * scale, low_masks)
            probs = probabilities(stacked, k_pad[window], tile, length).astype(BF16)
            mixed = pick_heads(mm(probs, v_pad[window]), masks)
            position = lax.broadcasted_iota(jnp.int32, mixed.shape, 0) + tile * TILE
            mixed = jnp.where(position >= length + WINDOW - 1, value_sum[...] * (1.0 / CLIP), mixed)
            heads_out[rows] = mixed.astype(BF16)
        send[...] = heads_out[pl.ds(pl.multiple_of((1 - core) * HALF, HALF), HALF)]


def project_kernel(meta, own, arrived, w_own, w_other, out):
    out[...] = (mm(own[...], w_own[...]) + mm(arrived[...], w_other[...])).astype(BF16)


def attend_back_kernel(
    first, meta, gh_own, gh_other, q_ref, k_ref, v_ref, cos_ref, sin_ref,
    grads, send, k_pad, v_pad, dk, dv, gh, dq,
):
    step = pl.program_id(0)
    core = meta[0]
    length = meta[1 + first + step]
    width = q_ref.shape[1]
    edge = jnp.zeros((TILE, width), BF16)
    for pad, source in ((k_pad, k_ref), (v_pad, v_ref)):
        pad[:TILE] = edge
        pad[TILE + CLIP :] = edge
        pad[TILE : TILE + CLIP] = source[...]
    dk[...] = jnp.zeros_like(dk)
    dv[...] = jnp.zeros_like(dv)
    for source, part in ((gh_own, core), (gh_other, 1 - core)):
        gh[pl.ds(pl.multiple_of(part * HALF, HALF), HALF)] = source[...]
    low_masks = lane_masks(width, BF16)
    masks = lane_masks(width, F32)
    scale = jnp.asarray(HEAD ** -0.5, BF16)
    for tile in range(CLIP // TILE):
        rows = slice(tile * TILE, (tile + 1) * TILE)
        window = slice(tile * TILE, tile * TILE + SPAN)
        stacked = stack_heads(q_ref[rows] * scale, low_masks)
        grad_out = stack_heads(gh[rows], low_masks)
        probs = probabilities(stacked, k_pad[window], tile, length)
        grad_probs = mm_t(grad_out, v_pad[window])
        inner = jnp.sum(probs * grad_probs, axis=-1, keepdims=True)
        grad_scores = (probs * (grad_probs - inner)).astype(BF16)
        dq[rows] = pick_heads(mm(grad_scores, k_pad[window]), masks) * HEAD ** -0.5
        dk[window] += t_mm(grad_scores, stacked)
        dv[window] += t_mm(probs.astype(BF16), grad_out)
    cosine = wide(cos_ref[...], width)
    sine = wide(sin_ref[...], width)
    inside = slice(TILE, TILE + CLIP)
    grad = dq[...]
    grads[:, :width] = (grad * cosine - swap_halves(grad) * sine).astype(BF16)
    grad = dk[inside]
    grads[:, width : 2 * width] = (grad * cosine - swap_halves(grad) * sine).astype(BF16)
    grads[:, 2 * width :] = dv[inside].astype(BF16)
    send[...] = grads[pl.ds(pl.multiple_of((1 - core) * HALF, HALF), HALF)]


def term_kernel(meta, own, arrived, x_ref, w_own, w_other, out, sums):
    width = w_own.shape[2]
    term = jnp.zeros(out.shape, F32)
    for grads, weight in ((own, w_own), (arrived, w_other)):
        for index in range(3):
            term = term + mm_t(grads[:, index * width : (index + 1) * width], weight[index])
    low = term.astype(BF16)
    out[...] = low
    term = low.astype(F32)
    scaled, _ = normalize(x_ref[...].astype(F32))

    @pl.when(pl.program_id(0) == 0)
    def _():
        sums[...] = jnp.zeros_like(sums)

    sums[0:1] += jnp.sum(term * scaled, axis=0, keepdims=True)
    sums[1:2] += jnp.sum(term, axis=0, keepdims=True)


def feed_kernel(first, count, meta, own, other, scale_one, gain, bias, scale_two, *refs):
    xs, cots = refs[:count], refs[count : 2 * count]
    w_in, w_in_other, w_down, w_down_other = refs[2 * count : 2 * count + 4]
    kept, sent, rows_out, gn_out, ff_out, sums, ff_acc, gn_acc = refs[2 * count + 4 :]
    step = pl.program_id(0)
    steps = pl.num_programs(0)
    pieces = [slice(clip * HALF, (clip + 1) * HALF) for clip in range(count)]

    def grad_two(clip):
        grad = cots[clip][...].astype(F32)
        position = lax.broadcasted_iota(jnp.int32, grad.shape, 0) + meta[0] * HALF
        return jnp.where(position < meta[1 + first + clip], grad, 0.0)

    @pl.when(step == 0)
    def _():
        for clip, rows in enumerate(pieces):
            attention = own[rows].astype(F32) + other[rows].astype(F32)
            hidden = xs[clip][...].astype(F32) + scale_one[...] * attention
            scaled, _ = normalize(hidden)
            rows_out[0, rows] = (scaled * gain[...] + bias[...]).astype(BF16)
            rows_out[1, rows] = (grad_two(clip) * scale_two[...]).astype(BF16)
        ff_acc[...] = jnp.zeros_like(ff_acc)
        gn_acc[...] = jnp.zeros_like(gn_acc)

    def units(w_in, w_down, hidden):
        low = rows_out[0]
        for start in range(0, w_down.shape[0], 256):
            part = slice(start, start + 256)
            gate = mm(low, w_in[0, :, part])
            up = mm(low, w_in[1, :, part])
            grad_act = mm_t(rows_out[1], w_down[part])
            sg = 1.0 / (1.0 + jnp.exp(-gate))
            silu = gate * sg
            hidden[2, :, part] = (silu * up).astype(BF16)
            hidden[0, :, part] = (grad_act * up * (sg + silu * (1.0 - sg))).astype(BF16)
            hidden[1, :, part] = (grad_act * silu).astype(BF16)
        ff_acc[...] += mm(hidden[2], w_down[...])
        gn_acc[...] += mm_t(hidden[0], w_in[0]) + mm_t(hidden[1], w_in[1])

    @pl.when(step < steps // 2)
    def _():
        units(w_in, w_down, kept)

    @pl.when(step >= steps // 2)
    def _():
        units(w_in_other, w_down_other, sent)

    @pl.when(step == steps - 1)
    def _():
        sums[...] = jnp.zeros_like(sums)
        gn_out[...] = gn_acc[...].astype(BF16)
        for clip, rows in enumerate(pieces):
            low = ff_acc[rows].astype(BF16)
            ff_out[rows] = low
            sums[0:1] += jnp.sum(low.astype(F32) * grad_two(clip), axis=0, keepdims=True)


def valid(first, meta, dims):
    position = lax.broadcasted_iota(jnp.int32, dims, 0) + meta[0] * HALF
    return position < meta[1 + first + pl.program_id(0)]


def middle_back_kernel(
    first, meta, own, other, g_own, g_other, x_ref, cot, scale_one, gain, w_out, w_other,
    grad_out, low_out, gh_out, gh_send, sums,
):
    attention = own[...].astype(F32) + other[...].astype(F32)
    hidden = x_ref[...].astype(F32) + scale_one[...] * attention
    scaled, inverse = normalize(hidden)
    grad_normed = g_own[...].astype(F32) + g_other[...].astype(F32)
    grad_two = jnp.where(valid(first, meta, cot.shape), cot[...].astype(F32), 0.0)
    grad_one = grad_two + norm_back(grad_normed, scaled, inverse, gain[...])
    grad_out[...] = grad_one
    low = (grad_one * scale_one[...]).astype(BF16)
    low_out[...] = low
    gh_out[...] = mm_t(low, w_out[...]).astype(BF16)
    gh_send[...] = mm_t(low, w_other[...]).astype(BF16)

    @pl.when(pl.program_id(0) == 0)
    def _():
        sums[...] = jnp.zeros_like(sums)

    sums[0:1] += jnp.sum(grad_one * attention, axis=0, keepdims=True)
    sums[1:2] += jnp.sum(grad_normed * scaled, axis=0, keepdims=True)
    sums[2:3] += jnp.sum(grad_normed, axis=0, keepdims=True)


def output_kernel(first, meta, own, other, f_own, f_other, x_ref, scale_one, scale_two, out):
    attention = own[...].astype(F32) + other[...].astype(F32)
    hidden = x_ref[...].astype(F32) + scale_one[...] * attention
    result = hidden + scale_two[...] * (f_own[...].astype(F32) + f_other[...].astype(F32))
    out[...] = jnp.where(valid(first, meta, result.shape), result, 0.0).astype(BF16)


def input_back_kernel(first, meta, g_own, g_other, grad_one, x_ref, gain, out):
    scaled, inverse = normalize(x_ref[...].astype(F32))
    grad_normed = g_own[...].astype(F32) + g_other[...].astype(F32)
    out[...] = (grad_one[...] + norm_back(grad_normed, scaled, inverse, gain[...])).astype(BF16)


def place_kernel(meta, own, other, *refs):
    out = refs[-1]
    for source, part in ((own, meta[0]), (other, 1 - meta[0])):
        out[pl.ds(pl.multiple_of(part * HALF, HALF), HALF)] = source[...]


def sum_kernel(keep, arrived, out):
    out[...] = (keep[...].astype(F32) + arrived[...].astype(F32)).astype(BF16)


def final_kernel(own, *refs):
    qkv, out = refs[3:]
    width = out.shape[0]
    for index in range(4):
        columns = slice(index * width, (index + 1) * width)
        value = own[:, columns].astype(F32)
        for piece in refs[:3]:
            value = value + piece[:, columns].astype(F32)
        if index < 3:
            qkv[index] = value
        else:
            out[...] = value.T


def final_turned_kernel(own, *refs):
    value = own[...].astype(F32)
    for piece in refs[:3]:
        value = value + piece[...].astype(F32)
    refs[3][...] = value.T


def weight_grad_kernel(lefts, rights, first_steps, by_halves, parted, meta, order, *refs):
    count = sum(lefts)
    left = refs[:count]
    right = refs[count : count + sum(rights)]
    outs = refs[count + sum(rights) : -2]
    rows, result = refs[-2:]
    step = pl.program_id(0)

    def gather(pieces):
        start = 0
        for piece in pieces:
            size = piece.shape[-2]
            rows[start : start + size] = piece[0] if len(piece.shape) == 3 else piece[...]
            start += size

    def multiply(pieces):
        product = t_mm(rows[...], jnp.concatenate(pieces, axis=0)).astype(BF16)
        if not parted:
            outs[0][...] = product
            return
        result[...] = product
        slices = product.shape[0] // 128
        for spot in range(slices):
            out = outs[spot // (slices // 2)]
            spot_in = spot % (slices // 2) * 128
            out[spot_in : spot_in + 128] = result[
                pl.ds(pl.multiple_of(order[spot] * 128, 128), 128)
            ]

    def flat(piece):
        return piece[0] if len(piece.shape) == 3 else piece[...]

    def split(piece):
        halves = []
        for part in (meta[0], 1 - meta[0]):
            for clip in range(piece.shape[0] // CLIP):
                halves.append(piece[pl.ds(pl.multiple_of(clip * CLIP + part * HALF, HALF), HALF)])
        return halves

    @pl.when(step == 0)
    def _():
        gather(left[: lefts[0]])

    if first_steps is None:
        multiply([flat(piece) for piece in right])
        return

    @pl.when(step == first_steps)
    def _():
        gather(left[lefts[0] :])

    @pl.when(step < first_steps)
    def _():
        multiply([flat(piece) for piece in right[: rights[0]]])

    @pl.when(step >= first_steps)
    def _():
        if by_halves:
            multiply([half for piece in right[rights[0] :] for half in split(piece)])
        else:
            multiply([flat(piece) for piece in right[rights[0] :]])


def shape(rows, columns, dtype=BF16):
    return jax.ShapeDtypeStruct((rows, columns), dtype)


def stored(*dims):
    return pltpu.HBM(dims, BF16)


def whole(*dims):
    return pl.BlockSpec(dims, lambda i, *_: (0,) * len(dims), pipeline_mode=pl.Buffered(1))


def total(*dims):
    return pl.BlockSpec(dims, lambda i, *_: (0,) * len(dims))


def smem():
    return pl.BlockSpec(memory_space=pltpu.SMEM)


def call(
    body, limit, inputs, in_specs, out_specs, out_shape, grid, scratch, us, after=(), prefetch=0,
    aliases={}, vector=None, through=(),
):
    count = len(inputs)
    extra = len(after)
    small = [] if vector is None else list(vector)
    through = list(through)
    outs = len(out_shape)
    aliases = dict(aliases)

    def kernel(*refs):
        arrays = refs[:count]
        left = refs[count : count + len(small)]
        rest = list(refs[count + len(small) + len(through) + extra :])
        del rest[outs + len(small) // 2 : outs + len(small) // 2 + len(through)]
        if small:
            summed = rest.pop(outs)

            @pl.when(pl.program_id(0) == 0)
            def _():
                summed[...] = left[0][...] + left[1][...]

        body(*arrays, *rest)

    out_specs, out_shape = list(out_specs), list(out_shape)
    in_specs = list(in_specs)
    if small:
        in_specs += [total(*small[0].shape)] * 2
        out_specs.append(total(*small[0].shape))
        out_shape.append(jax.ShapeDtypeStruct(small[0].shape, F32))
    for index, array in enumerate(through):
        aliases[count + len(small) + index] = len(out_shape)
        out_specs.append(pl.BlockSpec(memory_space=pl.ANY))
        out_shape.append(jax.ShapeDtypeStruct(array.shape, array.dtype))
    return pl.pallas_call(
        kernel,
        grid_spec=pltpu.PrefetchScalarGridSpec(
            num_scalar_prefetch=prefetch,
            grid=grid,
            in_specs=in_specs + [pl.BlockSpec(memory_space=pl.ANY)] * (len(through) + extra),
            out_specs=out_specs,
            scratch_shapes=scratch,
        ),
        out_shape=out_shape,
        name=getattr(body, "func", body).__name__[:-7],
        compiler_params=pltpu.CompilerParams(vmem_limit_bytes=limit * MIB),
        cost_estimate=pl.CostEstimate(
            flops=int(us * 1.0e9) + 1, bytes_accessed=128, transcendentals=0
        ),
        input_output_aliases=aliases,
    )(*inputs, *small, *through, *after)


def weight_grad(run, meta, order, limit, first, second, block, parted=True):
    specs, arrays, lefts, rights, steps = [], [], [], [], []
    products = [first] if second is None else [first, second]
    for left, _, _ in products:
        lefts.append(len(left))
        for array, group in left:
            arrays.append(array)
            if group is None:
                specs.append(whole(*array.shape))
            else:
                specs.append(
                    pl.BlockSpec(
                        (1, *array.shape[1:]), lambda i, group=group: (group, 0, 0),
                        pipeline_mode=pl.Buffered(1),
                    )
                )
    start = 0
    for _, right, groups in products:
        rights.append(len(right))
        count = right[0].shape[-1] // block
        total_steps = count * (1 if groups is None else len(groups))

        def at(i, start=start, total_steps=total_steps):
            return jnp.clip(i - start, 0, total_steps - 1)

        for array in right:
            arrays.append(array)
            rows = array.shape[-2]
            if groups is None:
                specs.append(pl.BlockSpec((rows, block), lambda i, at=at: (0, at(i))))
            else:
                specs.append(
                    pl.BlockSpec(
                        (1, rows, block),
                        lambda i, at=at, groups=groups, count=count: (
                            groups[0] + at(i) // count, 0, at(i) % count
                        ),
                    )
                )
        steps.append(total_steps)
        start += total_steps
    depth = first[0][0][0].shape[-1]
    rows = sum(array.shape[-2] for array, _ in first[0])
    out = pl.BlockSpec((depth // 2, block), lambda i: (0, i))
    return run(
        functools.partial(
            weight_grad_kernel, lefts, rights, None if second is None else steps[0],
            second is not None and second[2] is None, parted,
        ),
        limit,
        [meta, order, *arrays],
        [smem(), smem()] + specs,
        [out] * 2 if parted else [pl.BlockSpec((depth, block), lambda i: (0, i))],
        [shape(depth // 2, start * block)] * 2 if parted else [shape(depth, start * block)],
        (start,),
        [pltpu.VMEM((rows, depth), BF16), pltpu.VMEM((depth, block), BF16)], 20.0,
    )


def build(dp_size, chunks_of):
    cos_np, sin_np = tables()

    def per_device(
        inputs, cotangent, lengths, first_gain, first_bias, qkv_weight, out_weight, first_scale,
        second_gain, second_bias, in_weight, down_weight, second_scale,
    ):
        chunks = chunks_of(lengths.shape[0])
        depth = inputs.shape[1]
        width = out_weight.shape[0]
        units = down_weight.shape[0]
        place = lax.axis_index("tensor")
        spot = lax.axis_index("dp")
        core = place % 2
        meta = jnp.concatenate([core.reshape(1).astype(jnp.int32), lengths])
        natural = jnp.arange(depth // 128, dtype=jnp.int32)
        if dp_size == 8:
            y, z = spot % 2, spot // 2
            order = jnp.stack(
                [2 * (z ^ hop) + y for hop in range(4)] + [2 * (z ^ hop) + 1 - y for hop in range(4)]
            ).astype(jnp.int32)
        else:
            order = natural
        cos_t = jnp.asarray(cos_np)
        sin_t = jnp.asarray(sin_np)
        row = lambda v: v.reshape(1, depth)
        first_gain, first_bias, first_scale = row(first_gain), row(first_bias), row(first_scale)
        second_gain, second_bias, second_scale = row(second_gain), row(second_bias), row(second_scale)

        chain, pending, arriving, summed, held = [], [], [], [], []

        def run(*arguments, **named):
            if pending:
                named["vector"] = pending.pop()
                arriving.clear()
            results = call(
                *arguments, after=tuple(chain), through=[at[key] for at, key in held], **named
            )
            chain[:] = [results[0]]
            results = list(results)
            for at, key in reversed(held):
                at[key] = results.pop()
            held.clear()
            if "vector" in named:
                summed[:] = [results.pop()]
            return results

        def swap(values, bit):
            return lax.ppermute(values, "tensor", [(i, i ^ bit) for i in range(4)])

        out_other, in_other, down_other, qkv_other = (
            swap(weight, 1) for weight in (out_weight, in_weight, down_weight, qkv_weight)
        )
        half_rows = pl.BlockSpec((HALF, depth), lambda i, *m: (i, 0))
        half_head = pl.BlockSpec((HALF, width), lambda i, *m: (i, 0))
        own_head = pl.BlockSpec((HALF, width), lambda i, m: (2 * i + m[0], 0))
        clip_head = pl.BlockSpec((CLIP, width), lambda i, *m: (i, 0))

        def own_rows(first):
            return pl.BlockSpec((HALF, depth), lambda i, m: (2 * (first + i) + m[0], 0))

        def attend(chunk):
            first, count = chunk[0], len(chunk)
            pad = pltpu.VMEM((CLIP + 2 * TILE, width), BF16)
            return run(
                functools.partial(attend_kernel, first),
                60,
                [meta, inputs, first_gain, first_bias, qkv_weight, cos_t, sin_t],
                [
                    smem(), pl.BlockSpec((HALF, depth), lambda i: (2 * first + i, 0)), whole(1, depth),
                    whole(1, depth), whole(3, depth, width), whole(CLIP, 128), whole(CLIP, 128),
                ],
                [
                    half_rows, half_head, half_head, half_head,
                    pl.BlockSpec((CLIP, width), lambda i: (i // 2, 0)),
                    pl.BlockSpec((HALF, width), lambda i: (i // 2, 0)),
                ],
                [stored(count * CLIP, depth)] + [stored(count * CLIP, width)] * 4
                + [shape(count * HALF, width)],
                (2 * count,),
                [pltpu.VMEM((CLIP, width), BF16), pad, pad, pltpu.VMEM((1, width), F32)], 0.0 * count,
            )

        def project(chunk, heads, arrived):
            return run(
                project_kernel, 60,
                [meta, heads, arrived, out_weight, out_other],
                [own_head, half_head, whole(width, depth), whole(width, depth)],
                [half_rows], [shape(len(chunk) * HALF, depth)], (len(chunk),), [], 0.0 * len(chunk), prefetch=1,
            )[0]

        def feed(chunk, own, other):
            first, count = chunk[0], len(chunk)
            block = 512
            steps = units // block
            rows = count * HALF
            mine = lambda i: jnp.minimum(i, steps - 1)
            theirs = lambda i: jnp.maximum(i - steps, 0)
            local = [
                pl.BlockSpec(
                    (HALF, depth), lambda i, m, c=c: (2 * c + m[0], 0), pipeline_mode=pl.Buffered(1)
                )
                for c in chunk
            ]
            hidden = jax.ShapeDtypeStruct((3, rows, units), BF16)
            return run(
                functools.partial(feed_kernel, first, count),
                60,
                [meta, own, other, first_scale, second_gain, second_bias, second_scale]
                + [inputs] * count + [cotangent] * count
                + [in_weight, in_other, down_weight, down_other],
                [whole(rows, depth)] * 2 + [whole(1, depth)] * 4 + local + local
                + [
                    pl.BlockSpec((2, depth, block), lambda i, m: (0, 0, mine(i))),
                    pl.BlockSpec((2, depth, block), lambda i, m: (0, 0, theirs(i))),
                    pl.BlockSpec((block, depth), lambda i, m: (mine(i), 0)),
                    pl.BlockSpec((block, depth), lambda i, m: (theirs(i), 0)),
                ],
                [
                    pl.BlockSpec((3, rows, block), lambda i, m: (0, 0, mine(i))),
                    pl.BlockSpec((3, rows, block), lambda i, m: (0, 0, theirs(i))),
                    whole(2, rows, depth), whole(rows, depth), whole(rows, depth), total(8, depth),
                ],
                [
                    stored(3, rows, units), hidden, jax.ShapeDtypeStruct((2, rows, depth), BF16),
                    shape(rows, depth), shape(rows, depth), shape(8, depth, F32),
                ],
                (2 * steps,),
                [pltpu.VMEM((rows, depth), F32)] * 2, 15.0 * count,
                prefetch=1,
            )

        def middle_back(chunk, own, other, g_own, g_other):
            first, count = chunk[0], len(chunk)
            rows = count * HALF
            return run(
                functools.partial(middle_back_kernel, first),
                60,
                [
                    meta, own, other, g_own, g_other, inputs, cotangent, first_scale, second_gain,
                    out_weight, out_other,
                ],
                [half_rows] * 4 + [own_rows(first)] * 2 + [whole(1, depth)] * 2
                + [whole(width, depth)] * 2,
                [half_rows, half_rows, half_head, half_head, total(8, depth)],
                [
                    shape(rows, depth, F32), shape(rows, depth), shape(rows, width),
                    shape(rows, width), shape(8, depth, F32),
                ],
                (count,), [], 60.0 * count, prefetch=1,
            )

        def attend_back(chunk, own, other, q, k, v):
            first, count = chunk[0], len(chunk)
            pad = (CLIP + 2 * TILE, width)
            return run(
                functools.partial(attend_back_kernel, first),
                60,
                [meta, own, other, q, k, v, cos_t, sin_t],
                [
                    smem(), half_head, half_head, clip_head, clip_head, clip_head,
                    whole(CLIP, 128), whole(CLIP, 128),
                ],
                [
                    pl.BlockSpec((CLIP, 3 * width), lambda i: (i, 0)),
                    pl.BlockSpec((HALF, 3 * width), lambda i: (i, 0)),
                ],
                [stored(count * CLIP, 3 * width), shape(count * HALF, 3 * width)],
                (count,),
                [
                    pltpu.VMEM(pad, BF16), pltpu.VMEM(pad, BF16), pltpu.VMEM(pad, F32),
                    pltpu.VMEM(pad, F32), pltpu.VMEM((CLIP, width), BF16),
                    pltpu.VMEM((CLIP, width), F32),
                ], 15.0 * count,
            )

        def first_term(chunk, grads, arrived):
            first, count = chunk[0], len(chunk)
            return run(
                term_kernel, 60,
                [meta, grads, arrived, inputs, qkv_weight, qkv_other],
                [
                    pl.BlockSpec((HALF, 3 * width), lambda i, m: (2 * i + m[0], 0)),
                    pl.BlockSpec((HALF, 3 * width), lambda i, m: (i, 0)), own_rows(first),
                    whole(3, depth, width), whole(3, depth, width),
                ],
                [half_rows, total(8, depth)],
                [shape(count * HALF, depth), shape(8, depth, F32)],
                (count,), [], 15.0 * count, prefetch=1,
            )

        def rowwise(body, chunk, local, shared):
            first, count = chunk[0], len(chunk)
            return run(
                functools.partial(body, first),
                60,
                [meta, *local, inputs, *shared],
                [half_rows] * len(local) + [own_rows(first)] + [whole(1, depth)] * len(shared),
                [half_rows], [shape(count * HALF, depth)], (count,), [], 15.0 * count, prefetch=1,
            )[0]

        def put(chunk, own, other, base):
            first, count = chunk[0], len(chunk)
            extra = [] if base is None else [base]
            return run(
                place_kernel,
                60,
                [meta, own, other, *extra],
                [smem(), half_rows, half_rows] + [pl.BlockSpec(memory_space=pl.ANY)] * len(extra),
                [pl.BlockSpec((CLIP, depth), lambda i: (first + i, 0))],
                [shape(inputs.shape[0], depth)],
                (count,), [], 15.0, aliases={} if base is None else {3: 0},
            )[0]

        def scatter_y(keep, send):
            if dp_size != 8:
                whole_grad = jnp.concatenate([keep, send], axis=0)
                result = lax.psum_scatter(whole_grad, "dp", scatter_dimension=0, tiled=True)
                return lambda: result
            arrived = lax.ppermute(send, "dp", [(i, i ^ 1) for i in range(8)])
            rows, columns = keep.shape
            part = pl.BlockSpec((rows, 512), lambda i: (0, i))
            return lambda: run(
                sum_kernel, 60, [keep, arrived], [part, part], [part], [shape(rows, columns)],
                (columns // 512,), [], 15.0,
            )[0]

        def send_z(pair):
            return [pair] + [
                lax.ppermute(
                    pair[hop * 128 : (hop + 1) * 128], "dp", [(i, i ^ (2 * hop)) for i in range(8)]
                )
                for hop in (1, 2, 3)
            ]

        def final(pieces):
            if dp_size != 8:
                value = pieces.astype(F32)
                qkv = jnp.stack([value[:, i * width : (i + 1) * width] for i in range(3)])
                return qkv, value[:, 3 * width :].T
            piece = whole(128, 4 * width)
            return run(
                final_kernel, 60, pieces, [piece] * 4, [total(3, 128, width), total(width, 128)],
                [jax.ShapeDtypeStruct((3, 128, width), F32), shape(width, 128, F32)], (1,), [], 15.0,
            )

        def final_turned(pieces):
            if dp_size != 8:
                return pieces.astype(F32).T
            columns = pieces[0].shape[1]
            block = 512
            part = pl.BlockSpec((128, block), lambda i: (0, i))
            return run(
                final_turned_kernel, 60, pieces, [part] * 4,
                [pl.BlockSpec((block, 128), lambda i: (i, 0))], [shape(columns, 128, F32)],
                (columns // block,), [], 15.0,
            )[0]

        def scatter_z(pair):
            if dp_size != 8:
                return pair.astype(F32)
            total_sum = pair[:128].astype(F32)
            for hop in (1, 2, 3):
                piece = pair[hop * 128 : (hop + 1) * 128]
                piece = lax.ppermute(piece, "dp", [(i, i ^ (2 * hop)) for i in range(8)])
                total_sum = total_sum + piece.astype(F32)
            return total_sum

        state = [dict() for _ in chunks]
        parts = list(zip(chunks, state))

        def tail_output(chunk, at, base):
            own = rowwise(
                output_kernel, chunk, [at["own"], at["other"], at["ff"], at["ff_other"]],
                [first_scale, second_scale],
            )
            other = swap(own, 1)
            return lambda: put(chunk, own, other, base)

        def tail_input(chunk, at, base):
            own = rowwise(
                input_back_kernel, chunk, [at["g1"], at["g1_other"], at["grad_one"]], [first_gain]
            )
            other = swap(own, 1)
            return lambda: put(chunk, own, other, base)

        def forward(chunk, at):
            at["normed"], at["q"], at["k"], at["v"], at["heads"], send = attend(chunk)
            at["heads_other"] = swap(send, 1)

        def projected(chunk, at):
            at["own"] = project(chunk, at["heads"], at["heads_other"])
            at["other"] = swap(at["own"], 2)

        def fed(chunk, at):
            at["kept"], send, at["rows"], at["gn"], at["ff"], at["feed_sums"] = feed(
                chunk, at["own"], at["other"]
            )
            at["gn_other"] = swap(at["gn"], 2)
            at["arrived"] = swap(send, 1)
            at["rows_other"] = swap(at["rows"], 1)

        def middle(chunk, at):
            at["grad_one"], at["ga"], at["gh"], send, at["mid_sums"] = middle_back(
                chunk, at["own"], at["other"], at["gn"], at["gn_other"]
            )
            at["gh_other"] = swap(send, 1)
            at["ga_other"] = swap(at["ga"], 1)

        def back(chunk, at):
            at["dqkv"], send = attend_back(
                chunk, at["gh"], at["gh_other"], at["q"], at["k"], at["v"]
            )
            at["dqkv_other"] = swap(send, 1)

        def term(chunk, at):
            at["g1"], at["term_sums"] = first_term(chunk, at["dqkv"], at["dqkv_other"])
            at["g1_other"] = swap(at["g1"], 2)

        def vectors():
            alike = sum(at["mid_sums"] for at in state)[0:3]
            backward = sum(at["term_sums"] for at in state)[0:2]
            forward = sum(at["feed_sums"] for at in state)[0:1]
            alike = jnp.where(place < 2, alike, 0.0)
            return jnp.concatenate([backward, alike, forward, jnp.zeros((2, depth), F32)], axis=0)

        hops = []
        while 2 ** len(hops) < dp_size:
            hops.append(("dp", 2 ** len(hops)))
        hops += [("tensor", 1), ("tensor", 2)]

        def hop(values):
            axis, bit = hops.pop(0)
            count = 4 if axis == "tensor" else dp_size
            arriving[:] = [(values, lax.ppermute(values, axis, [(i, i ^ bit) for i in range(count)]))]

        def send_forward(at):
            at["ff_other"] = swap(at["ff"], 2)

        output, input_grad = None, None
        forward(*parts[0])
        projected(*parts[0])
        forward(*parts[1])
        projected(*parts[1])
        fed(*parts[0])
        fed(*parts[1])
        n_pieces = [(at[key], 0) for at in state for key in ("rows", "rows_other")]
        gf_pieces = [(at[key], 1) for at in state for key in ("rows", "rows_other")]
        right = [at[key] for at in state for key in ("kept", "arrived")]
        middle(*parts[0])
        held.append((state[0], "ff"))
        (grads_in,) = weight_grad(
            run, meta, natural, 60, (n_pieces, right, (0, 1)), None, 512, False
        )
        in_sum = lax.psum_scatter(grads_in, "dp", scatter_dimension=0, tiled=True).astype(F32)
        gate_sum, up_sum = in_sum[:, :units], in_sum[:, units:]
        send_forward(state[0])
        back(*parts[0])
        down_sum = scatter_y(
            *weight_grad(run, meta, order, 60, (gf_pieces, right, (2,)), None, 512)
        )
        term(*parts[0])
        held.append((state[1], "ff"))
        middle(*parts[1])
        send_forward(state[1])
        place_out_0 = tail_output(*parts[0], output)
        back(*parts[1])
        output = place_out_0()
        term(*parts[1])
        hop(vectors())
        attention_sum = scatter_y(
            *weight_grad(
                run, meta, order, 60,
                ([(at["normed"], None) for at in state], [at["dqkv"] for at in state], None),
                (
                    [(at[key], None) for at in state for key in ("ga", "ga_other")],
                    [at["heads"] for at in state], None,
                ),
                256,
            )
        )
        pending[:] = arriving
        place_in_0 = tail_input(*parts[0], input_grad)
        hop(summed[0])
        place_out_1 = tail_output(*parts[1], output)
        pending[:] = arriving
        input_grad = place_in_0()
        hop(summed[0])
        down_sum = down_sum()
        if dp_size == 8:
            down_sum = send_z(down_sum)
        pending[:] = arriving
        output = place_out_1()
        hop(summed[0])
        attention_sum = attention_sum()
        if dp_size == 8:
            attention_sum = send_z(attention_sum)
        pending[:] = arriving
        place_in_1 = tail_input(*parts[1], input_grad)
        hop(summed[0])
        down_sum = final_turned(down_sum)
        qkv_sum, out_sum = final(attention_sum)
        input_grad = place_in_1()

        if arriving and arriving[0][0] is summed[0]:
            summed[:] = [arriving[0][0] + arriving[0][1]]
        while hops:
            values = summed[0]
            axis, bit = hops.pop(0)
            count = 4 if axis == "tensor" else dp_size
            summed[:] = [values + lax.ppermute(values, axis, [(i, i ^ bit) for i in range(count)])]
        share = depth // dp_size
        mine = lax.dynamic_slice_in_dim(summed[0], spot * share, share, 1)

        return (
            output,
            input_grad,
            mine[0],
            mine[1],
            qkv_sum,
            out_sum,
            mine[2],
            mine[3],
            mine[4],
            jnp.stack([gate_sum, up_sum]),
            down_sum,
            mine[5],
        )

    return per_device


def in_chunks(clips):
    return [list(range(1)), list(range(1, clips))]


def solution(mesh):
    placed = (
        P("dp", None), P("dp", None), P("dp"), P(), P(), P(None, None, "tensor"),
        P("tensor", None), P(), P(), P(), P(None, None, "tensor"), P("tensor", None), P(),
    )
    return jax.shard_map(
        build(mesh.shape["dp"], in_chunks),
        mesh=mesh,
        in_specs=placed,
        out_specs=(
            P("dp", None), P("dp", None), P("dp"), P("dp"), P(None, "dp", "tensor"),
            P("tensor", "dp"), P("dp"), P("dp"), P("dp"), P(None, "dp", "tensor"),
            P("tensor", "dp"), P("dp"),
        ),
        check_vma=False,
    )
```

```python
import functools

import jax
import jax.numpy as jnp
import numpy as np
from jax import lax
from jax.experimental import pallas as pl
from jax.experimental.pallas import tpu as pltpu
from jax.sharding import PartitionSpec as P

HEAD = 64
WINDOW = 128
CLIP = 512
HALF = CLIP // 2
TILE = 128
SPAN = 3 * TILE
SLOT = 144
MIB = 1024 * 1024
F32 = jnp.float32
BF16 = jnp.bfloat16


def tables():
    half_size = HEAD // 2
    frequency = (10000.0 ** (-2.0 * np.arange(half_size, dtype=np.float32) / HEAD)).astype(np.float32)
    angles = np.arange(CLIP, dtype=np.float32)[:, None] * frequency[None, :]
    cosine = np.cos(angles).astype(np.float32)
    sine = np.sin(angles).astype(np.float32)
    return (
        np.concatenate([cosine, cosine] * 2, axis=1),
        np.concatenate([-sine, sine] * 2, axis=1),
    )


def mm(a, b):
    return lax.dot_general(a, b, (((1,), (0,)), ((), ())), preferred_element_type=F32)


def mm_t(a, b):
    return lax.dot_general(a, b, (((1,), (1,)), ((), ())), preferred_element_type=F32)


def t_mm(a, b):
    return lax.dot_general(a, b, (((0,), (0,)), ((), ())), preferred_element_type=F32)


def normalize(values):
    center = jnp.mean(values, axis=-1, keepdims=True)
    shifted = values - center
    spread = jnp.mean(shifted * shifted, axis=-1, keepdims=True)
    inverse = lax.rsqrt(spread + 1e-05)
    return shifted * inverse, inverse


def norm_back(grad_normed, scaled, inverse, gain):
    weighted = grad_normed * gain
    centered = weighted - jnp.mean(weighted, axis=-1, keepdims=True)
    return inverse * (centered - scaled * jnp.mean(weighted * scaled, axis=-1, keepdims=True))


def swap_halves(values):
    width = values.shape[1]
    lane = lax.broadcasted_iota(jnp.int32, values.shape, 1)
    up = pltpu.roll(values, width - HEAD // 2, 1)
    down = pltpu.roll(values, HEAD // 2, 1)
    return jnp.where(lane % HEAD < HEAD // 2, up, down)


def wide(table, width):
    return jnp.concatenate([table] * (width // table.shape[1]), axis=1)


def lane_masks(width, dtype):
    lane = lax.broadcasted_iota(jnp.int32, (1, width), 1) // HEAD
    return [(lane == head).astype(F32).astype(dtype) for head in range(width // HEAD)]


def stack_heads(rows, masks):
    return jnp.concatenate([rows * mask for mask in masks], axis=0)


def pick_heads(stacked, masks):
    total = stacked[:TILE] * masks[0]
    for head in range(1, len(masks)):
        total = total + stacked[head * TILE : (head + 1) * TILE] * masks[head]
    return total


def window_bias(rows):
    row = lax.broadcasted_iota(jnp.int32, (rows, SPAN), 0) % TILE
    ahead = lax.broadcasted_iota(jnp.int32, (rows, SPAN), 1) - row
    return jnp.where((ahead > 0) & (ahead < 2 * WINDOW), 0.0, -1e30)


def probabilities(queries, keys, tile, length, bias):
    key = lax.broadcasted_iota(jnp.int32, (1, SPAN), 1) + (tile - 1) * TILE
    outside = jnp.where((key >= 0) & (key < length), 0.0, -1e30)
    scores = mm_t(queries, keys) + bias[...] + outside
    maximum = jnp.max(scores, axis=-1, keepdims=True)
    weights = jnp.exp(scores - maximum)
    return weights * (1.0 / jnp.sum(weights, axis=-1, keepdims=True))


def attend_kernel(
    first, meta, x_ref, gain, bias, w_qkv, cos_ref, sin_ref,
    normed, q_out, k_out, v_out, heads_out, send, q_all, k_pad, v_pad, value_sum, bias_of,
):
    step = pl.program_id(0)
    half = step % 2
    core = meta[0]
    length = meta[1 + first + step // 2]
    width = w_qkv.shape[2]

    @pl.when(step == 0)
    def _():
        bias_of[...] = window_bias(bias_of.shape[0])
        edge = jnp.zeros((TILE, width), BF16)
        for pad in (k_pad, v_pad):
            pad[:TILE] = edge
            pad[TILE + CLIP :] = edge

    scaled, _ = normalize(x_ref[...].astype(F32))
    low = (scaled * gain[...] + bias[...]).astype(BF16)
    normed[...] = low
    rows = pl.ds(pl.multiple_of(half * HALF, HALF), HALF)
    inside = pl.ds(pl.multiple_of(half * HALF + TILE, TILE), HALF)
    cosine = wide(cos_ref[rows], width)
    sine = wide(sin_ref[rows], width)
    queries = mm(low, w_qkv[0])
    queries = (queries * cosine + swap_halves(queries) * sine).astype(BF16)
    q_out[...] = queries
    q_all[rows] = queries
    keys = mm(low, w_qkv[1])
    keys = (keys * cosine + swap_halves(keys) * sine).astype(BF16)
    k_out[...] = keys
    k_pad[inside] = keys
    values = mm(low, w_qkv[2]).astype(BF16)
    v_out[...] = values
    v_pad[inside] = values
    total = jnp.sum(values.astype(F32), axis=0, keepdims=True)
    value_sum[...] = jnp.where(half == 0, total, value_sum[...] + total)

    @pl.when(half == 1)
    def _():
        low_masks = lane_masks(width, BF16)
        masks = lane_masks(width, F32)
        scale = jnp.asarray(HEAD ** -0.5, BF16)
        for tile in range(CLIP // TILE):
            rows = slice(tile * TILE, (tile + 1) * TILE)
            window = slice(tile * TILE, tile * TILE + SPAN)
            stacked = stack_heads(q_all[rows] * scale, low_masks)
            probs = probabilities(stacked, k_pad[window], tile, length, bias_of).astype(BF16)
            mixed = pick_heads(mm(probs, v_pad[window]), masks)
            position = lax.broadcasted_iota(jnp.int32, mixed.shape, 0) + tile * TILE
            mixed = jnp.where(position >= length + WINDOW - 1, value_sum[...] * (1.0 / CLIP), mixed)
            heads_out[rows] = mixed.astype(BF16)
        send[...] = heads_out[pl.ds(pl.multiple_of((1 - core) * HALF, HALF), HALF)]


def project_kernel(meta, own, arrived, w_own, w_other, out):
    out[...] = (mm(own[...], w_own[...]) + mm(arrived[...], w_other[...])).astype(BF16)


def attend_back_kernel(
    first, meta, gh_own, gh_other, q_ref, k_ref, v_ref, cos_ref, sin_ref,
    grads, send, k_pad, v_pad, dk, dv, gh, dq, bias_of,
):
    step = pl.program_id(0)
    core = meta[0]
    length = meta[1 + first + step]
    width = q_ref.shape[1]

    @pl.when(step == 0)
    def _():
        bias_of[...] = window_bias(bias_of.shape[0])

    edge = jnp.zeros((TILE, width), BF16)
    for pad, source in ((k_pad, k_ref), (v_pad, v_ref)):
        pad[:TILE] = edge
        pad[TILE + CLIP :] = edge
        pad[TILE : TILE + CLIP] = source[...]
    dk[...] = jnp.zeros_like(dk)
    dv[...] = jnp.zeros_like(dv)
    for source, part in ((gh_own, core), (gh_other, 1 - core)):
        gh[pl.ds(pl.multiple_of(part * HALF, HALF), HALF)] = source[...]
    low_masks = lane_masks(width, BF16)
    masks = lane_masks(width, F32)
    scale = jnp.asarray(HEAD ** -0.5, BF16)
    for tile in range(CLIP // TILE):
        rows = slice(tile * TILE, (tile + 1) * TILE)
        window = slice(tile * TILE, tile * TILE + SPAN)
        stacked = stack_heads(q_ref[rows] * scale, low_masks)
        grad_out = stack_heads(gh[rows], low_masks)
        probs = probabilities(stacked, k_pad[window], tile, length, bias_of)
        grad_probs = mm_t(grad_out, v_pad[window])
        inner = jnp.sum(probs * grad_probs, axis=-1, keepdims=True)
        grad_scores = (probs * (grad_probs - inner)).astype(BF16)
        dq[rows] = pick_heads(mm(grad_scores, k_pad[window]), masks) * HEAD ** -0.5
        dk[window] += t_mm(grad_scores, stacked)
        dv[window] += t_mm(probs.astype(BF16), grad_out)
    cosine = wide(cos_ref[...], width)
    sine = wide(sin_ref[...], width)
    inside = slice(TILE, TILE + CLIP)
    grad = dq[...]
    grads[:, :width] = (grad * cosine - swap_halves(grad) * sine).astype(BF16)
    grad = dk[inside]
    grads[:, width : 2 * width] = (grad * cosine - swap_halves(grad) * sine).astype(BF16)
    grads[:, 2 * width :] = dv[inside].astype(BF16)
    send[...] = grads[pl.ds(pl.multiple_of((1 - core) * HALF, HALF), HALF)]


def term_kernel(meta, own, arrived, x_ref, w_own, w_other, out, sums):
    width = w_own.shape[2]
    term = jnp.zeros(out.shape, F32)
    for grads, weight in ((own, w_own), (arrived, w_other)):
        for index in range(3):
            term = term + mm_t(grads[:, index * width : (index + 1) * width], weight[index])
    low = term.astype(BF16)
    out[...] = low
    term = low.astype(F32)
    scaled, _ = normalize(x_ref[...].astype(F32))

    @pl.when(pl.program_id(0) == 0)
    def _():
        sums[...] = jnp.zeros_like(sums)

    sums[0:1] += jnp.sum(term * scaled, axis=0, keepdims=True)
    sums[1:2] += jnp.sum(term, axis=0, keepdims=True)


def feed_kernel(first, count, meta, own, other, scale_one, gain, bias, scale_two, *refs):
    xs, cots = refs[:count], refs[count : 2 * count]
    own_in, other_in, own_down, other_down = refs[2 * count : 2 * count + 4]
    kept, sent, rows_out, gn_out, ff_out, sums, ff_acc, gn_acc, in_buf, down_buf, sems = refs[
        2 * count + 4 :
    ]
    block = down_buf.shape[1]
    step = pl.program_id(0)
    steps = pl.num_programs(0)
    pieces = [slice(clip * HALF, (clip + 1) * HALF) for clip in range(count)]

    def copies(w_in, w_down, index, slot):
        part = pl.ds(pl.multiple_of(index * block, block), block)
        return (
            pltpu.make_async_copy(w_in.at[:, :, part], in_buf.at[slot], sems.at[0, slot]),
            pltpu.make_async_copy(w_down.at[part], down_buf.at[slot], sems.at[1, slot]),
        )

    def fetch(index):
        slot = index % 2

        @pl.when(index < steps // 2)
        def _():
            for copy in copies(own_in, own_down, index, slot):
                copy.start()

        @pl.when(index >= steps // 2)
        def _():
            for copy in copies(other_in, other_down, index - steps // 2, slot):
                copy.start()

    @pl.when(step == 0)
    def _():
        fetch(0)

    @pl.when(step + 1 < steps)
    def _():
        fetch(step + 1)

    def grad_two(clip):
        grad = cots[clip][...].astype(F32)
        position = lax.broadcasted_iota(jnp.int32, grad.shape, 0) + meta[0] * HALF
        return jnp.where(position < meta[1 + first + clip], grad, 0.0)

    @pl.when(step == 0)
    def _():
        for clip, rows in enumerate(pieces):
            attention = own[rows].astype(F32) + other[rows].astype(F32)
            hidden = xs[clip][...].astype(F32) + scale_one[...] * attention
            scaled, _ = normalize(hidden)
            rows_out[0, rows] = (scaled * gain[...] + bias[...]).astype(BF16)
            rows_out[1, rows] = (grad_two(clip) * scale_two[...]).astype(BF16)
        ff_acc[...] = jnp.zeros_like(ff_acc)
        gn_acc[...] = jnp.zeros_like(gn_acc)

    for copy in copies(own_in, own_down, 0, step % 2):
        copy.wait()

    def units(hidden):
        w_in, w_down = in_buf.at[step % 2], down_buf.at[step % 2]
        low = rows_out[0]
        for start in range(0, w_down.shape[0], 256):
            part = slice(start, start + 256)
            gate = mm(low, w_in[0, :, part])
            up = mm(low, w_in[1, :, part])
            grad_act = mm_t(rows_out[1], w_down[part])
            sg = 1.0 / (1.0 + jnp.exp(-gate))
            silu = gate * sg
            hidden[2, :, part] = (silu * up).astype(BF16)
            hidden[0, :, part] = (grad_act * up * (sg + silu * (1.0 - sg))).astype(BF16)
            hidden[1, :, part] = (grad_act * silu).astype(BF16)
        ff_acc[...] += mm(hidden[2], w_down[...])
        gn_acc[...] += mm_t(hidden[0], w_in[0]) + mm_t(hidden[1], w_in[1])

    @pl.when(step < steps // 2)
    def _():
        units(kept)

    @pl.when(step >= steps // 2)
    def _():
        units(sent)
        width = block
        for index in range(2):
            for start in range(0, rows_out.shape[2], width):

                @pl.when(step - steps // 2 == start // width)
                def _():
                    sent[3 + index] = rows_out[index, :, start : start + width]

    @pl.when(step == steps - 1)
    def _():
        sums[...] = jnp.zeros_like(sums)
        gn_out[...] = gn_acc[...].astype(BF16)
        for clip, rows in enumerate(pieces):
            low = ff_acc[rows].astype(BF16)
            ff_out[rows] = low
            sums[0:1] += jnp.sum(low.astype(F32) * grad_two(clip), axis=0, keepdims=True)


def valid(first, meta, dims):
    position = lax.broadcasted_iota(jnp.int32, dims, 0) + meta[0] * HALF
    return position < meta[1 + first + pl.program_id(0)]


def middle_back_kernel(
    first, meta, own, other, g_own, g_other, x_ref, cot, scale_one, gain, w_out, w_other,
    grad_out, low_out, gh_out, send, sums,
):
    attention = own[...].astype(F32) + other[...].astype(F32)
    hidden = x_ref[...].astype(F32) + scale_one[...] * attention
    scaled, inverse = normalize(hidden)
    grad_normed = g_own[...].astype(F32) + g_other[...].astype(F32)
    grad_two = jnp.where(valid(first, meta, cot.shape), cot[...].astype(F32), 0.0)
    grad_one = grad_two + norm_back(grad_normed, scaled, inverse, gain[...])
    grad_out[...] = grad_one
    low = (grad_one * scale_one[...]).astype(BF16)
    low_out[...] = low
    gh_out[...] = mm_t(low, w_out[...]).astype(BF16)
    send[:, : low.shape[1]] = low
    send[:, low.shape[1] :] = mm_t(low, w_other[...]).astype(BF16)

    @pl.when(pl.program_id(0) == 0)
    def _():
        sums[...] = jnp.zeros_like(sums)

    sums[0:1] += jnp.sum(grad_one * attention, axis=0, keepdims=True)
    sums[1:2] += jnp.sum(grad_normed * scaled, axis=0, keepdims=True)
    sums[2:3] += jnp.sum(grad_normed, axis=0, keepdims=True)


def finish_kernel(
    first, meta, own, other, f_own, f_other, g_own, g_other, grad_one, x_ref, scale_one, scale_two,
    gain, out,
):
    residual = x_ref[...].astype(F32)
    attention = own[...].astype(F32) + other[...].astype(F32)
    hidden = residual + scale_one[...] * attention
    result = hidden + scale_two[...] * (f_own[...].astype(F32) + f_other[...].astype(F32))
    out[0] = jnp.where(valid(first, meta, result.shape), result, 0.0).astype(BF16)
    scaled, inverse = normalize(residual)
    grad_normed = g_own[...].astype(F32) + g_other[...].astype(F32)
    out[1] = (grad_one[...] + norm_back(grad_normed, scaled, inverse, gain[...])).astype(BF16)


def place_kernel(meta, own, other, *refs):
    for group, out in enumerate(refs[-2:]):
        for source, part in ((own, meta[0]), (other, 1 - meta[0])):
            out[pl.ds(pl.multiple_of(part * HALF, HALF), HALF)] = source[group]


def sum_kernel(keep, arrived, out):
    out[...] = (keep[...].astype(F32) + arrived[...].astype(F32)).astype(BF16)


def sum_rider_kernel(keep, arrived, out):
    for start in range(0, out.shape[0], SLOT):
        rows = slice(start, start + 128)
        out[rows] = (keep[rows].astype(F32) + arrived[rows].astype(F32)).astype(BF16)
        rows = slice(start + 128, start + SLOT)
        both = keep[rows].astype(F32) + arrived[rows].astype(F32)
        value = both[:8] + both[8:]
        high = value.astype(BF16).astype(F32)
        out[rows] = jnp.concatenate([high, value - high], axis=0).astype(BF16)


def final_kernel(own, *refs):
    qkv, out, vectors = refs[3:]
    width = qkv.shape[2]
    for index in range(4):
        columns = slice(index * width, (index + 1) * width)
        value = own[:, columns].astype(F32)
        for piece in refs[:3]:
            value = value + piece[:, columns].astype(F32)
        if index < 3:
            qkv[index] = value[:128]
        else:
            out[...] = value[:128].T
        if index == 0:
            vectors[...] = value[128:136, :128] + value[136:, :128]


def final_turned_kernel(own, *refs):
    value = own[...].astype(F32)
    for piece in refs[:3]:
        value = value + piece[...].astype(F32)
    refs[3][...] = value.T


def widen_kernel(total, out):
    columns = out.shape[2]
    for index in range(out.shape[0]):
        out[index] = total[:, index * columns : (index + 1) * columns].astype(F32)


def weight_grad_kernel(lefts, rights, first_steps, by_halves, parted, meta, order, *refs, rider=False):
    count = sum(lefts)
    left = refs[:count]
    right = refs[count : count + sum(rights)]
    vectors = refs[count + sum(rights)] if rider else None
    outs = refs[count + sum(rights) + int(rider) : -2]
    rows, result = refs[-2:]
    slot = SLOT if rider else 128
    step = pl.program_id(0)

    def gather(pieces):
        start = 0
        for piece in pieces:
            size = piece.shape[-2]
            rows[start : start + size] = piece[0] if len(piece.shape) == 3 else piece[...]
            start += size

    def multiply(pieces):
        product = t_mm(rows[...], jnp.concatenate(pieces, axis=0)).astype(BF16)
        if not parted:
            outs[0][...] = product
            return
        result[...] = product
        slices = product.shape[0] // 128
        for spot in range(slices):
            out = outs[spot // (slices // 2)]
            start = spot % (slices // 2) * slot
            from_row = pl.multiple_of(order[spot] * 128, 128)
            out[start : start + 128] = result[pl.ds(from_row, 128)]
            if rider:
                value = vectors[:, pl.ds(from_row, 128)]
                high = value.astype(BF16).astype(F32)
                both = jnp.concatenate([high, value - high], axis=0)
                both = jnp.concatenate([both, jnp.zeros_like(both)], axis=1)
                out[start + 128 : start + slot] = both.astype(BF16)

    def flat(piece):
        return piece[0] if len(piece.shape) == 3 else piece[...]

    def split(piece):
        halves = []
        for part in (meta[0], 1 - meta[0]):
            for clip in range(piece.shape[0] // CLIP):
                halves.append(piece[pl.ds(pl.multiple_of(clip * CLIP + part * HALF, HALF), HALF)])
        return halves

    @pl.when(step == 0)
    def _():
        gather(left[: lefts[0]])

    if first_steps is None:
        multiply([flat(piece) for piece in right])
        return

    @pl.when(step == first_steps)
    def _():
        gather(left[lefts[0] :])

    @pl.when(step < first_steps)
    def _():
        multiply([flat(piece) for piece in right[: rights[0]]])

    @pl.when(step >= first_steps)
    def _():
        if by_halves:
            multiply([half for piece in right[rights[0] :] for half in split(piece)])
        else:
            multiply([flat(piece) for piece in right[rights[0] :]])


def shape(rows, columns, dtype=BF16):
    return jax.ShapeDtypeStruct((rows, columns), dtype)


def stored(*dims):
    return pltpu.HBM(dims, BF16)


def whole(*dims):
    return pl.BlockSpec(dims, lambda i, *_: (0,) * len(dims), pipeline_mode=pl.Buffered(1))


def total(*dims):
    return pl.BlockSpec(dims, lambda i, *_: (0,) * len(dims))


def smem():
    return pl.BlockSpec(memory_space=pltpu.SMEM)


def call(
    body, limit, inputs, in_specs, out_specs, out_shape, grid, scratch, us, after=(), prefetch=0,
    aliases={}, through=(),
):
    count = len(inputs)
    extra = len(after)
    through = list(through)
    outs = len(out_shape)
    aliases = dict(aliases)

    def kernel(*refs):
        results = refs[count + len(through) + extra :]
        body(*refs[:count], *results[:outs], *results[outs + len(through) :])

    out_specs, out_shape = list(out_specs), list(out_shape)
    in_specs = list(in_specs)
    for index, array in enumerate(through):
        aliases[count + index] = len(out_shape)
        out_specs.append(pl.BlockSpec(memory_space=pl.ANY))
        out_shape.append(jax.ShapeDtypeStruct(array.shape, array.dtype))
    return pl.pallas_call(
        kernel,
        grid_spec=pltpu.PrefetchScalarGridSpec(
            num_scalar_prefetch=prefetch,
            grid=grid,
            in_specs=in_specs + [pl.BlockSpec(memory_space=pl.ANY)] * (len(through) + extra),
            out_specs=out_specs,
            scratch_shapes=scratch,
        ),
        out_shape=out_shape,
        name=getattr(body, "func", body).__name__[:-7],
        compiler_params=pltpu.CompilerParams(vmem_limit_bytes=limit * MIB),
        cost_estimate=pl.CostEstimate(
            flops=int(us * 1.0e9) + 1, bytes_accessed=128, transcendentals=0
        ),
        input_output_aliases=aliases,
    )(*inputs, *through, *after)


def weight_grad(run, meta, order, limit, first, second, block, parted=True, rider=None):
    depth = first[0][0][0].shape[-1]
    specs, arrays, lefts, rights, steps = [], [], [], [], []
    products = [first] if second is None else [first, second]
    for left, _, _ in products:
        lefts.append(len(left))
        for array, group in left:
            arrays.append(array)
            if group is None:
                specs.append(whole(array.shape[0], depth))
            else:
                specs.append(
                    pl.BlockSpec(
                        (1, *array.shape[1:]), lambda i, group=group: (group, 0, 0),
                        pipeline_mode=pl.Buffered(1),
                    )
                )
    start = 0
    for _, right, groups in products:
        rights.append(len(right))
        count = right[0].shape[-1] // block
        total_steps = count * (1 if groups is None else len(groups))

        def at(i, start=start, total_steps=total_steps):
            return jnp.clip(i - start, 0, total_steps - 1)

        for array in right:
            arrays.append(array)
            rows = array.shape[-2]
            if groups is None:
                specs.append(pl.BlockSpec((rows, block), lambda i, at=at: (0, at(i))))
            else:
                specs.append(
                    pl.BlockSpec(
                        (1, rows, block),
                        lambda i, at=at, groups=groups, count=count: (
                            groups[0] + at(i) // count, 0, at(i) % count
                        ),
                    )
                )
        steps.append(total_steps)
        start += total_steps
    height = depth // 2
    if rider is not None:
        arrays.append(rider)
        specs.append(whole(*rider.shape))
        height = depth // 256 * SLOT
    rows = sum(array.shape[-2] for array, _ in first[0])
    out = pl.BlockSpec((height, block), lambda i: (0, i))
    return run(
        functools.partial(
            weight_grad_kernel, lefts, rights, None if second is None else steps[0],
            second is not None and second[2] is None, parted, rider=rider is not None,
        ),
        limit,
        [meta, order, *arrays],
        [smem(), smem()] + specs,
        [out] * 2 if parted else [pl.BlockSpec((depth, block), lambda i: (0, i))],
        [shape(height, start * block)] * 2 if parted else [shape(depth, start * block)],
        (start,),
        [pltpu.VMEM((rows, depth), BF16), pltpu.VMEM((depth, block), BF16)], 20.0,
    )


def build(dp_size, chunks_of):
    cos_np, sin_np = tables()

    def per_device(
        inputs, cotangent, lengths, first_gain, first_bias, qkv_weight, out_weight, first_scale,
        second_gain, second_bias, in_weight, down_weight, second_scale,
    ):
        chunks = chunks_of(lengths.shape[0])
        depth = inputs.shape[1]
        width = out_weight.shape[0]
        units = down_weight.shape[0]
        place = lax.axis_index("tensor")
        spot = lax.axis_index("dp")
        core = place % 2
        meta = jnp.concatenate([core.reshape(1).astype(jnp.int32), lengths])
        natural = jnp.arange(depth // 128, dtype=jnp.int32)
        if dp_size == 8:
            y, z = spot % 2, spot // 2
            order = jnp.stack(
                [2 * (z ^ hop) + y for hop in range(4)] + [2 * (z ^ hop) + 1 - y for hop in range(4)]
            ).astype(jnp.int32)
        else:
            order = natural
        cos_t = jnp.asarray(cos_np)
        sin_t = jnp.asarray(sin_np)
        row = lambda v: v.reshape(1, depth)
        first_gain, first_bias, first_scale = row(first_gain), row(first_bias), row(first_scale)
        second_gain, second_bias, second_scale = row(second_gain), row(second_bias), row(second_scale)

        chain, held = [], []

        def run(*arguments, **named):
            results = call(
                *arguments, after=tuple(chain), through=[at[key] for at, key in held], **named
            )
            chain[:] = [results[0]]
            results = list(results)
            for at, key in reversed(held):
                at[key] = results.pop()
            held.clear()
            return results

        def swap(values, bit):
            return lax.ppermute(values, "tensor", [(i, i ^ bit) for i in range(4)])

        out_other, in_other, down_other, qkv_other = (
            swap(weight, 1) for weight in (out_weight, in_weight, down_weight, qkv_weight)
        )
        half_rows = pl.BlockSpec((HALF, depth), lambda i, *m: (i, 0))
        half_head = pl.BlockSpec((HALF, width), lambda i, *m: (i, 0))
        own_head = pl.BlockSpec((HALF, width), lambda i, m: (2 * i + m[0], 0))
        clip_head = pl.BlockSpec((CLIP, width), lambda i, *m: (i, 0))

        def own_rows(first):
            return pl.BlockSpec((HALF, depth), lambda i, m: (2 * (first + i) + m[0], 0))

        def attend(chunk):
            first, count = chunk[0], len(chunk)
            pad = pltpu.VMEM((CLIP + 2 * TILE, width), BF16)
            return run(
                functools.partial(attend_kernel, first),
                63,
                [meta, inputs, first_gain, first_bias, qkv_weight, cos_t, sin_t],
                [
                    smem(), pl.BlockSpec((HALF, depth), lambda i: (2 * first + i, 0)), whole(1, depth),
                    whole(1, depth), whole(3, depth, width), whole(CLIP, 128), whole(CLIP, 128),
                ],
                [
                    half_rows, half_head, half_head, half_head,
                    pl.BlockSpec((CLIP, width), lambda i: (i // 2, 0)),
                    pl.BlockSpec((HALF, width), lambda i: (i // 2, 0)),
                ],
                [stored(count * CLIP, depth)] + [stored(count * CLIP, width)] * 4
                + [shape(count * HALF, width)],
                (2 * count,),
                [
                    pltpu.VMEM((CLIP, width), BF16), pad, pad, pltpu.VMEM((1, width), F32),
                    pltpu.VMEM((width // HEAD * TILE, SPAN), F32),
                ], 0.0 * count,
            )

        def project(chunk, heads, arrived):
            return run(
                project_kernel, 63,
                [meta, heads, arrived, out_weight, out_other],
                [own_head, half_head, whole(width, depth), whole(width, depth)],
                [half_rows], [shape(len(chunk) * HALF, depth)], (len(chunk),), [], 0.0 * len(chunk), prefetch=1,
            )[0]

        def feed(chunk, own, other):
            first, count = chunk[0], len(chunk)
            block = 512
            steps = units // block
            rows = count * HALF
            mine = lambda i: jnp.minimum(i, steps - 1)
            theirs = lambda i: jnp.maximum(i - steps, 0)
            local = [
                pl.BlockSpec(
                    (HALF, depth), lambda i, m, c=c: (2 * c + m[0], 0), pipeline_mode=pl.Buffered(1)
                )
                for c in chunk
            ]
            hidden = jax.ShapeDtypeStruct((5, rows, units), BF16)
            return run(
                functools.partial(feed_kernel, first, count),
                63,
                [meta, own, other, first_scale, second_gain, second_bias, second_scale]
                + [inputs] * count + [cotangent] * count
                + [in_weight, in_other, down_weight, down_other],
                [whole(rows, depth)] * 2 + [whole(1, depth)] * 4 + local + local
                + [
                    pl.BlockSpec(memory_space=pl.ANY) for _ in range(4)
                ],
                [
                    pl.BlockSpec((3, rows, block), lambda i, m: (0, 0, mine(i))),
                    pl.BlockSpec((5, rows, block), lambda i, m: (0, 0, theirs(i))),
                    whole(2, rows, depth), whole(rows, depth), whole(rows, depth), total(8, depth),
                ],
                [
                    stored(3, rows, units), hidden, jax.ShapeDtypeStruct((2, rows, depth), BF16),
                    shape(rows, depth), shape(rows, depth), shape(8, depth, F32),
                ],
                (2 * steps,),
                [pltpu.VMEM((rows, depth), F32)] * 2
                + [
                    pltpu.VMEM((2, 2, depth, block), BF16), pltpu.VMEM((2, block, depth), BF16),
                    pltpu.SemaphoreType.DMA((2, 2)),
                ], 15.0 * count,
                prefetch=1,
            )

        def middle_back(chunk, own, other, g_own, g_other):
            first, count = chunk[0], len(chunk)
            rows = count * HALF
            return run(
                functools.partial(middle_back_kernel, first),
                63,
                [
                    meta, own, other, g_own, g_other, inputs, cotangent, first_scale, second_gain,
                    out_weight, out_other,
                ],
                [half_rows] * 4 + [own_rows(first)] * 2 + [whole(1, depth)] * 2
                + [whole(width, depth)] * 2,
                [
                    half_rows, half_rows, half_head,
                    pl.BlockSpec((HALF, depth + width), lambda i, m: (i, 0)), total(8, depth),
                ],
                [
                    shape(rows, depth, F32), shape(rows, depth), shape(rows, width),
                    shape(rows, depth + width), shape(8, depth, F32),
                ],
                (count,), [], 200.0 if first == 0 else 10.0, prefetch=1,
            )

        def attend_back(chunk, own, other, q, k, v):
            first, count = chunk[0], len(chunk)
            pad = (CLIP + 2 * TILE, width)
            return run(
                functools.partial(attend_back_kernel, first),
                63,
                [meta, own, other, q, k, v, cos_t, sin_t],
                [
                    smem(), half_head,
                    pl.BlockSpec((HALF, width), lambda i: (i, depth // width)), clip_head, clip_head, clip_head,
                    whole(CLIP, 128), whole(CLIP, 128),
                ],
                [
                    pl.BlockSpec((CLIP, 3 * width), lambda i: (i, 0)),
                    pl.BlockSpec((HALF, 3 * width), lambda i: (i, 0)),
                ],
                [stored(count * CLIP, 3 * width), shape(count * HALF, 3 * width)],
                (count,),
                [
                    pltpu.VMEM(pad, BF16), pltpu.VMEM(pad, BF16), pltpu.VMEM(pad, F32),
                    pltpu.VMEM(pad, F32), pltpu.VMEM((CLIP, width), BF16),
                    pltpu.VMEM((CLIP, width), F32), pltpu.VMEM((width // HEAD * TILE, SPAN), F32),
                ], 12.0 * count,
            )

        def first_term(chunk, grads, arrived):
            first, count = chunk[0], len(chunk)
            return run(
                term_kernel, 63,
                [meta, grads, arrived, inputs, qkv_weight, qkv_other],
                [
                    pl.BlockSpec((HALF, 3 * width), lambda i, m: (2 * i + m[0], 0)),
                    pl.BlockSpec((HALF, 3 * width), lambda i, m: (i, 0)), own_rows(first),
                    whole(3, depth, width), whole(3, depth, width),
                ],
                [half_rows, total(8, depth)],
                [shape(count * HALF, depth), shape(8, depth, F32)],
                (count,), [], 12.0 * count, prefetch=1,
            )

        def finish(chunk, local, shared):
            first, count = chunk[0], len(chunk)
            return run(
                functools.partial(finish_kernel, first),
                63,
                [meta, *local, inputs, *shared],
                [half_rows] * len(local) + [own_rows(first)] + [whole(1, depth)] * len(shared),
                [pl.BlockSpec((2, HALF, depth), lambda i, m: (0, i, 0))],
                [jax.ShapeDtypeStruct((2, count * HALF, depth), BF16)], (count,), [],
                12.0, prefetch=1,
            )[0]

        def put(chunk, own, other, bases):
            first, count = chunk[0], len(chunk)
            part = pl.BlockSpec((2, HALF, depth), lambda i: (0, i, 0))
            return run(
                place_kernel,
                63,
                [meta, own, other, *bases],
                [smem(), part, part] + [pl.BlockSpec(memory_space=pl.ANY)] * len(bases),
                [pl.BlockSpec((CLIP, depth), lambda i: (first + i, 0))] * 2,
                [shape(inputs.shape[0], depth)] * 2,
                (count,), [], 8.0, aliases={3: 0, 4: 1} if bases else {},
            )

        def scatter_y(keep, send, body=sum_kernel):
            if dp_size != 8:
                whole_grad = jnp.concatenate([keep, send], axis=0)
                result = lax.psum_scatter(whole_grad, "dp", scatter_dimension=0, tiled=True)
                return lambda: result
            arrived = lax.ppermute(send, "dp", [(i, i ^ 1) for i in range(8)])
            rows, columns = keep.shape
            block = columns // (2 if columns % 512 == 0 else 1)
            part = pl.BlockSpec((rows, block), lambda i: (0, i))
            return lambda: run(
                body, 63, [keep, arrived], [part, part], [part], [shape(rows, columns)],
                (columns // block,), [], 8.0,
            )[0]

        def send_z(pair):
            slot = pair.shape[0] // 4
            return [pair] + [
                lax.ppermute(
                    pair[hop * slot : (hop + 1) * slot], "dp", [(i, i ^ (2 * hop)) for i in range(8)]
                )
                for hop in (1, 2, 3)
            ]

        def final(pieces):
            if dp_size != 8:
                value = pieces.astype(F32)
                qkv = jnp.stack([value[:, i * width : (i + 1) * width] for i in range(3)])
                return qkv, value[:, 3 * width :].T, None
            return run(
                final_kernel, 63, pieces, [whole(SLOT, 4 * width)] * 4,
                [total(3, 128, width), total(width, 128), total(8, 128)],
                [
                    jax.ShapeDtypeStruct((3, 128, width), F32), shape(width, 128, F32),
                    shape(8, 128, F32),
                ],
                (1,), [], 8.0,
            )

        def widen(value):
            rows = value.shape[0]
            return run(
                widen_kernel, 63, [value], [whole(rows, 2 * units)], [total(2, rows, units)],
                [jax.ShapeDtypeStruct((2, rows, units), F32)], (1,), [], 8.0,
            )[0]

        def final_turned(pieces):
            if dp_size != 8:
                return (pieces.astype(F32).T,)
            return run(
                final_turned_kernel, 63, pieces, [whole(128, units)] * 4, [total(units, 128)],
                [shape(units, 128, F32)], (1,), [], 8.0,
            )

        state = [dict() for _ in chunks]
        parts = list(zip(chunks, state))

        def ending(chunk, at):
            own = finish(
                chunk,
                [
                    at["own"], at["other"], at["ff"], at["ff_other"], at["g1"], at["g1_other"],
                    at["grad_one"],
                ],
                [first_scale, second_scale, first_gain],
            )
            other = swap(own, 1)
            return lambda bases: put(chunk, own, other, bases)

        def forward(chunk, at):
            at["normed"], at["q"], at["k"], at["v"], at["heads"], send = attend(chunk)
            at["heads_other"] = swap(send, 1)

        def projected(chunk, at):
            at["own"] = project(chunk, at["heads"], at["heads_other"])
            at["other"] = swap(at["own"], 2)

        def fed(chunk, at):
            at["kept"], send, at["rows"], at["gn"], at["ff"], at["feed_sums"] = feed(
                chunk, at["own"], at["other"]
            )
            at["gn_other"] = swap(at["gn"], 2)
            at["arrived"] = swap(send, 1)

        def middle(chunk, at):
            at["grad_one"], at["ga"], at["gh"], send, at["mid_sums"] = middle_back(
                chunk, at["own"], at["other"], at["gn"], at["gn_other"]
            )
            at["back_other"] = swap(send, 1)

        def back(chunk, at):
            at["dqkv"], send = attend_back(
                chunk, at["gh"], at["back_other"], at["q"], at["k"], at["v"]
            )
            at["dqkv_other"] = swap(send, 1)

        def term(chunk, at):
            at["g1"], at["term_sums"] = first_term(chunk, at["dqkv"], at["dqkv_other"])
            at["g1_other"] = swap(at["g1"], 2)

        def vectors():
            alike = sum(at["mid_sums"] for at in state)[0:3]
            backward = sum(at["term_sums"] for at in state)[0:2]
            forward = sum(at["feed_sums"] for at in state)[0:1]
            alike = jnp.where(place < 2, alike, 0.0)
            return jnp.concatenate([backward, alike, forward, jnp.zeros((2, depth), F32)], axis=0)

        def send_forward(at):
            at["ff_other"] = swap(at["ff"], 2)

        results = []
        forward(*parts[0])
        projected(*parts[0])
        forward(*parts[1])
        chain.extend([in_other, down_other, qkv_other])
        projected(*parts[1])
        fed(*parts[0])
        fed(*parts[1])
        n_pieces = [piece for at in state for piece in ((at["rows"], 0), (at["arrived"], 3))]
        gf_pieces = [piece for at in state for piece in ((at["rows"], 1), (at["arrived"], 4))]
        right = [at[key] for at in state for key in ("kept", "arrived")]
        middle(*parts[0])
        held.append((state[0], "ff"))
        (grads_in,) = weight_grad(
            run, meta, natural, 63, (n_pieces, right, (0, 1)), None, 512, False
        )
        in_sum = lax.psum_scatter(grads_in, "dp", scatter_dimension=0, tiled=True)
        send_forward(state[0])
        back(*parts[0])
        turned_sum = scatter_y(
            *weight_grad(run, meta, order, 63, (gf_pieces, right, (2,)), None, 512)
        )
        middle(*parts[1])
        held.append((state[1], "ff"))
        term(*parts[0])
        send_forward(state[1])
        back(*parts[1])
        place_0 = ending(*parts[0])
        term(*parts[1])
        turned_sum = turned_sum()
        if dp_size == 8:
            turned_sum = send_z(turned_sum)
        stacked = vectors()
        qkv_sum = scatter_y(
            *weight_grad(
                run, meta, order, 63,
                ([(at["normed"], None) for at in state], [at["dqkv"] for at in state], None),
                (
                    [(at[key], None) for at in state for key in ("ga", "back_other")],
                    [at["heads"] for at in state], None,
                ),
                256, rider=stacked if dp_size == 8 else None,
            ),
            sum_rider_kernel,
        )
        results = place_0(results)
        place_1 = ending(*parts[1])
        qkv_sum = qkv_sum()
        if dp_size == 8:
            qkv_sum = send_z(qkv_sum)
        (down_sum,) = final_turned(turned_sum)
        in_sum = widen(in_sum)
        results = place_1(results)
        qkv_sum, out_sum, mine = final(qkv_sum)

        if dp_size != 8:
            bit = 1
            while bit < dp_size:
                stacked = stacked + lax.ppermute(
                    stacked, "dp", [(i, i ^ bit) for i in range(dp_size)]
                )
                bit *= 2
            share = depth // dp_size
            mine = lax.dynamic_slice_in_dim(stacked, spot * share, share, 1)
        mine = mine + sum(swap(mine, bit) for bit in (1, 2, 3))

        return (
            *results,
            mine[0],
            mine[1],
            qkv_sum,
            out_sum,
            mine[2],
            mine[3],
            mine[4],
            in_sum,
            down_sum,
            mine[5],
        )

    return per_device


def in_chunks(clips):
    return [list(range(1)), list(range(1, clips))]


def solution(mesh):
    placed = (
        P("dp", None), P("dp", None), P("dp"), P(), P(), P(None, None, "tensor"),
        P("tensor", None), P(), P(), P(), P(None, None, "tensor"), P("tensor", None), P(),
    )
    return jax.shard_map(
        build(mesh.shape["dp"], in_chunks),
        mesh=mesh,
        in_specs=placed,
        out_specs=(
            P("dp", None), P("dp", None), P("dp"), P("dp"), P(None, "dp", "tensor"),
            P("tensor", "dp"), P("dp"), P("dp"), P("dp"), P(None, "dp", "tensor"),
            P("tensor", "dp"), P("dp"),
        ),
        check_vma=False,
    )
```

```python
import functools

import jax
import jax.numpy as jnp
import numpy as np
from jax import lax
from jax.experimental import pallas as pl
from jax.experimental.pallas import tpu as pltpu
from jax.sharding import PartitionSpec as P

HEAD = 64
WINDOW = 128
CLIP = 512
HALF = CLIP // 2
TILE = 128
SPAN = 3 * TILE
SLOT = 144
MIB = 1024 * 1024
F32 = jnp.float32
BF16 = jnp.bfloat16


def tables():
    half_size = HEAD // 2
    frequency = (10000.0 ** (-2.0 * np.arange(half_size, dtype=np.float32) / HEAD)).astype(np.float32)
    angles = np.arange(CLIP, dtype=np.float32)[:, None] * frequency[None, :]
    cosine = np.cos(angles).astype(np.float32)
    sine = np.sin(angles).astype(np.float32)
    return (
        np.concatenate([cosine, cosine] * 2, axis=1),
        np.concatenate([-sine, sine] * 2, axis=1),
    )


def mm(a, b):
    return lax.dot_general(a, b, (((1,), (0,)), ((), ())), preferred_element_type=F32)


def mm_t(a, b):
    return lax.dot_general(a, b, (((1,), (1,)), ((), ())), preferred_element_type=F32)


def t_mm(a, b):
    return lax.dot_general(a, b, (((0,), (0,)), ((), ())), preferred_element_type=F32)


def normalize(values):
    center = jnp.mean(values, axis=-1, keepdims=True)
    shifted = values - center
    spread = jnp.mean(shifted * shifted, axis=-1, keepdims=True)
    inverse = lax.rsqrt(spread + 1e-05)
    return shifted * inverse, inverse


def norm_back(grad_normed, scaled, inverse, gain):
    weighted = grad_normed * gain
    centered = weighted - jnp.mean(weighted, axis=-1, keepdims=True)
    return inverse * (centered - scaled * jnp.mean(weighted * scaled, axis=-1, keepdims=True))


def swap_halves(values):
    width = values.shape[1]
    lane = lax.broadcasted_iota(jnp.int32, values.shape, 1)
    up = pltpu.roll(values, width - HEAD // 2, 1)
    down = pltpu.roll(values, HEAD // 2, 1)
    return jnp.where(lane % HEAD < HEAD // 2, up, down)


def wide(table, width):
    return jnp.concatenate([table] * (width // table.shape[1]), axis=1)


def lane_masks(width, dtype):
    lane = lax.broadcasted_iota(jnp.int32, (1, width), 1) // HEAD
    return [(lane == head).astype(F32).astype(dtype) for head in range(width // HEAD)]


def stack_heads(rows, masks):
    return jnp.concatenate([rows * mask for mask in masks], axis=0)


def pick_heads(stacked, masks):
    total = stacked[:TILE] * masks[0]
    for head in range(1, len(masks)):
        total = total + stacked[head * TILE : (head + 1) * TILE] * masks[head]
    return total


def window_bias(rows):
    row = lax.broadcasted_iota(jnp.int32, (rows, SPAN), 0) % TILE
    ahead = lax.broadcasted_iota(jnp.int32, (rows, SPAN), 1) - row
    return jnp.where((ahead > 0) & (ahead < 2 * WINDOW), 0.0, -1e30)


def probabilities(queries, keys, tile, length, bias):
    key = lax.broadcasted_iota(jnp.int32, (1, SPAN), 1) + (tile - 1) * TILE
    outside = jnp.where((key >= 0) & (key < length), 0.0, -1e30)
    scores = mm_t(queries, keys) + bias[...] + outside
    maximum = jnp.max(scores, axis=-1, keepdims=True)
    weights = jnp.exp(scores - maximum)
    return weights * (1.0 / jnp.sum(weights, axis=-1, keepdims=True))


def attend_kernel(
    first, meta, x_ref, gain, bias, w_qkv, cos_ref, sin_ref,
    normed, q_out, k_out, v_out, heads_out, send, q_all, k_pad, v_pad, value_sum, bias_of,
):
    step = pl.program_id(0)
    half = step % 2
    core = meta[0]
    length = meta[1 + first + step // 2]
    width = w_qkv.shape[2]

    @pl.when(step == 0)
    def _():
        bias_of[...] = window_bias(bias_of.shape[0])
        edge = jnp.zeros((TILE, width), BF16)
        for pad in (k_pad, v_pad):
            pad[:TILE] = edge
            pad[TILE + CLIP :] = edge

    scaled, _ = normalize(x_ref[...].astype(F32))
    low = (scaled * gain[...] + bias[...]).astype(BF16)
    normed[...] = low
    rows = pl.ds(pl.multiple_of(half * HALF, HALF), HALF)
    inside = pl.ds(pl.multiple_of(half * HALF + TILE, TILE), HALF)
    cosine = wide(cos_ref[rows], width)
    sine = wide(sin_ref[rows], width)
    queries = mm(low, w_qkv[0])
    queries = (queries * cosine + swap_halves(queries) * sine).astype(BF16)
    q_out[...] = queries
    q_all[rows] = queries
    keys = mm(low, w_qkv[1])
    keys = (keys * cosine + swap_halves(keys) * sine).astype(BF16)
    k_out[...] = keys
    k_pad[inside] = keys
    values = mm(low, w_qkv[2]).astype(BF16)
    v_out[...] = values
    v_pad[inside] = values
    total = jnp.sum(values.astype(F32), axis=0, keepdims=True)
    value_sum[...] = jnp.where(half == 0, total, value_sum[...] + total)

    @pl.when(half == 1)
    def _():
        low_masks = lane_masks(width, BF16)
        masks = lane_masks(width, F32)
        scale = jnp.asarray(HEAD ** -0.5, BF16)
        for tile in range(CLIP // TILE):
            rows = slice(tile * TILE, (tile + 1) * TILE)
            window = slice(tile * TILE, tile * TILE + SPAN)
            stacked = stack_heads(q_all[rows] * scale, low_masks)
            probs = probabilities(stacked, k_pad[window], tile, length, bias_of).astype(BF16)
            mixed = pick_heads(mm(probs, v_pad[window]), masks)
            position = lax.broadcasted_iota(jnp.int32, mixed.shape, 0) + tile * TILE
            mixed = jnp.where(position >= length + WINDOW - 1, value_sum[...] * (1.0 / CLIP), mixed)
            heads_out[rows] = mixed.astype(BF16)
        send[...] = heads_out[pl.ds(pl.multiple_of((1 - core) * HALF, HALF), HALF)]


def project_kernel(meta, own, arrived, w_own, w_other, out):
    out[...] = (mm(own[...], w_own[...]) + mm(arrived[...], w_other[...])).astype(BF16)


def attend_back_kernel(
    first, meta, gh_own, gh_other, q_ref, k_ref, v_ref, cos_ref, sin_ref,
    grads, send, k_pad, v_pad, dk, dv, gh, dq, bias_of,
):
    step = pl.program_id(0)
    core = meta[0]
    length = meta[1 + first + step]
    width = q_ref.shape[1]

    @pl.when(step == 0)
    def _():
        bias_of[...] = window_bias(bias_of.shape[0])

    edge = jnp.zeros((TILE, width), BF16)
    for pad, source in ((k_pad, k_ref), (v_pad, v_ref)):
        pad[:TILE] = edge
        pad[TILE + CLIP :] = edge
        pad[TILE : TILE + CLIP] = source[...]
    dk[...] = jnp.zeros_like(dk)
    dv[...] = jnp.zeros_like(dv)
    for source, part in ((gh_own, core), (gh_other, 1 - core)):
        gh[pl.ds(pl.multiple_of(part * HALF, HALF), HALF)] = source[...]
    low_masks = lane_masks(width, BF16)
    masks = lane_masks(width, F32)
    scale = jnp.asarray(HEAD ** -0.5, BF16)
    for tile in range(CLIP // TILE):
        rows = slice(tile * TILE, (tile + 1) * TILE)
        window = slice(tile * TILE, tile * TILE + SPAN)
        stacked = stack_heads(q_ref[rows] * scale, low_masks)
        grad_out = stack_heads(gh[rows], low_masks)
        probs = probabilities(stacked, k_pad[window], tile, length, bias_of)
        grad_probs = mm_t(grad_out, v_pad[window])
        inner = jnp.sum(probs * grad_probs, axis=-1, keepdims=True)
        grad_scores = (probs * (grad_probs - inner)).astype(BF16)
        dq[rows] = pick_heads(mm(grad_scores, k_pad[window]), masks) * HEAD ** -0.5
        dk[window] += t_mm(grad_scores, stacked)
        dv[window] += t_mm(probs.astype(BF16), grad_out)
    cosine = wide(cos_ref[...], width)
    sine = wide(sin_ref[...], width)
    inside = slice(TILE, TILE + CLIP)
    grad = dq[...]
    grads[:, :width] = (grad * cosine - swap_halves(grad) * sine).astype(BF16)
    grad = dk[inside]
    grads[:, width : 2 * width] = (grad * cosine - swap_halves(grad) * sine).astype(BF16)
    grads[:, 2 * width :] = dv[inside].astype(BF16)
    send[...] = grads[pl.ds(pl.multiple_of((1 - core) * HALF, HALF), HALF)]


def term_kernel(meta, own, arrived, x_ref, w_own, w_other, out, sums):
    width = w_own.shape[2]
    term = jnp.zeros(out.shape, F32)
    for grads, weight in ((own, w_own), (arrived, w_other)):
        for index in range(3):
            term = term + mm_t(grads[:, index * width : (index + 1) * width], weight[index])
    low = term.astype(BF16)
    out[...] = low
    term = low.astype(F32)
    scaled, _ = normalize(x_ref[...].astype(F32))

    @pl.when(pl.program_id(0) == 0)
    def _():
        sums[...] = jnp.zeros_like(sums)

    sums[0:1] += jnp.sum(term * scaled, axis=0, keepdims=True)
    sums[1:2] += jnp.sum(term, axis=0, keepdims=True)


def feed_kernel(first, count, meta, own, other, scale_one, gain, bias, scale_two, *refs):
    xs, cots = refs[:count], refs[count : 2 * count]
    own_in, other_in, own_down, other_down = refs[2 * count : 2 * count + 4]
    kept, sent, rows_out, gn_out, ff_out, sums, ff_acc, gn_acc, in_buf, down_buf, sems = refs[
        2 * count + 4 :
    ]
    block = down_buf.shape[1]
    step = pl.program_id(0)
    steps = pl.num_programs(0)
    pieces = [slice(clip * HALF, (clip + 1) * HALF) for clip in range(count)]

    def copies(w_in, w_down, index, slot):
        part = pl.ds(pl.multiple_of(index * block, block), block)
        return (
            pltpu.make_async_copy(w_in.at[:, :, part], in_buf.at[slot], sems.at[0, slot]),
            pltpu.make_async_copy(w_down.at[part], down_buf.at[slot], sems.at[1, slot]),
        )

    def fetch(index):
        slot = index % 2

        @pl.when(index < steps // 2)
        def _():
            for copy in copies(own_in, own_down, index, slot):
                copy.start()

        @pl.when(index >= steps // 2)
        def _():
            for copy in copies(other_in, other_down, index - steps // 2, slot):
                copy.start()

    @pl.when(step == 0)
    def _():
        fetch(0)

    @pl.when(step + 1 < steps)
    def _():
        fetch(step + 1)

    def grad_two(clip):
        grad = cots[clip][...].astype(F32)
        position = lax.broadcasted_iota(jnp.int32, grad.shape, 0) + meta[0] * HALF
        return jnp.where(position < meta[1 + first + clip], grad, 0.0)

    @pl.when(step == 0)
    def _():
        for clip, rows in enumerate(pieces):
            attention = own[rows].astype(F32) + other[rows].astype(F32)
            hidden = xs[clip][...].astype(F32) + scale_one[...] * attention
            scaled, _ = normalize(hidden)
            rows_out[0, rows] = (scaled * gain[...] + bias[...]).astype(BF16)
            rows_out[1, rows] = (grad_two(clip) * scale_two[...]).astype(BF16)
        ff_acc[...] = jnp.zeros_like(ff_acc)
        gn_acc[...] = jnp.zeros_like(gn_acc)

    for copy in copies(own_in, own_down, 0, step % 2):
        copy.wait()

    def units(hidden):
        w_in, w_down = in_buf.at[step % 2], down_buf.at[step % 2]
        low = rows_out[0]
        for start in range(0, w_down.shape[0], 256):
            part = slice(start, start + 256)
            gate = mm(low, w_in[0, :, part])
            up = mm(low, w_in[1, :, part])
            grad_act = mm_t(rows_out[1], w_down[part])
            sg = 1.0 / (1.0 + jnp.exp(-gate))
            silu = gate * sg
            hidden[2, :, part] = (silu * up).astype(BF16)
            hidden[0, :, part] = (grad_act * up * (sg + silu * (1.0 - sg))).astype(BF16)
            hidden[1, :, part] = (grad_act * silu).astype(BF16)
        ff_acc[...] += mm(hidden[2], w_down[...])
        gn_acc[...] += mm_t(hidden[0], w_in[0]) + mm_t(hidden[1], w_in[1])

    @pl.when(step < steps // 2)
    def _():
        units(kept)

    @pl.when(step >= steps // 2)
    def _():
        units(sent)
        width = block
        for index in range(2):
            for start in range(0, rows_out.shape[2], width):

                @pl.when(step - steps // 2 == start // width)
                def _():
                    sent[3 + index] = rows_out[index, :, start : start + width]

    @pl.when(step == steps - 1)
    def _():
        sums[...] = jnp.zeros_like(sums)
        gn_out[...] = gn_acc[...].astype(BF16)
        for clip, rows in enumerate(pieces):
            low = ff_acc[rows].astype(BF16)
            ff_out[rows] = low
            sums[0:1] += jnp.sum(low.astype(F32) * grad_two(clip), axis=0, keepdims=True)


def valid(first, meta, dims):
    position = lax.broadcasted_iota(jnp.int32, dims, 0) + meta[0] * HALF
    return position < meta[1 + first + pl.program_id(0)]


def middle_back_kernel(
    first, meta, own, other, g_own, g_other, x_ref, cot, scale_one, gain, w_out, w_other,
    grad_out, low_out, gh_out, send, sums,
):
    attention = own[...].astype(F32) + other[...].astype(F32)
    hidden = x_ref[...].astype(F32) + scale_one[...] * attention
    scaled, inverse = normalize(hidden)
    grad_normed = g_own[...].astype(F32) + g_other[...].astype(F32)
    grad_two = jnp.where(valid(first, meta, cot.shape), cot[...].astype(F32), 0.0)
    grad_one = grad_two + norm_back(grad_normed, scaled, inverse, gain[...])
    grad_out[...] = grad_one
    low = (grad_one * scale_one[...]).astype(BF16)
    low_out[...] = low
    gh_out[...] = mm_t(low, w_out[...]).astype(BF16)
    send[:, : low.shape[1]] = low
    send[:, low.shape[1] :] = mm_t(low, w_other[...]).astype(BF16)

    @pl.when(pl.program_id(0) == 0)
    def _():
        sums[...] = jnp.zeros_like(sums)

    sums[0:1] += jnp.sum(grad_one * attention, axis=0, keepdims=True)
    sums[1:2] += jnp.sum(grad_normed * scaled, axis=0, keepdims=True)
    sums[2:3] += jnp.sum(grad_normed, axis=0, keepdims=True)


def finish_kernel(
    first, meta, own, other, f_own, f_other, g_own, g_other, grad_one, x_ref, scale_one, scale_two,
    gain, out,
):
    residual = x_ref[...].astype(F32)
    attention = own[...].astype(F32) + other[...].astype(F32)
    hidden = residual + scale_one[...] * attention
    result = hidden + scale_two[...] * (f_own[...].astype(F32) + f_other[...].astype(F32))
    out[0] = jnp.where(valid(first, meta, result.shape), result, 0.0).astype(BF16)
    scaled, inverse = normalize(residual)
    grad_normed = g_own[...].astype(F32) + g_other[...].astype(F32)
    out[1] = (grad_one[...] + norm_back(grad_normed, scaled, inverse, gain[...])).astype(BF16)


def place_kernel(meta, own, other, *refs):
    for group, out in enumerate(refs[-2:]):
        for source, part in ((own, meta[0]), (other, 1 - meta[0])):
            out[pl.ds(pl.multiple_of(part * HALF, HALF), HALF)] = source[group]


def sum_kernel(keep, arrived, *outs):
    size = outs[0].shape[0]
    for index, out in enumerate(outs):
        rows = slice(index * size, (index + 1) * size)
        out[...] = (keep[rows].astype(F32) + arrived[rows].astype(F32)).astype(BF16)


def sum_rider_kernel(keep, arrived, *outs):
    for index, out in enumerate(outs):
        rows = slice(index * SLOT, index * SLOT + 128)
        out[:128] = (keep[rows].astype(F32) + arrived[rows].astype(F32)).astype(BF16)
        rows = slice(index * SLOT + 128, (index + 1) * SLOT)
        both = keep[rows].astype(F32) + arrived[rows].astype(F32)
        value = both[:8] + both[8:]
        high = value.astype(BF16).astype(F32)
        out[128:] = jnp.concatenate([high, value - high], axis=0).astype(BF16)


def final_kernel(own, *refs):
    qkv, out, vectors = refs[3:]
    width = qkv.shape[2]
    for index in range(4):
        columns = slice(index * width, (index + 1) * width)
        value = own[:, columns].astype(F32)
        for piece in refs[:3]:
            value = value + piece[:, columns].astype(F32)
        if index < 3:
            qkv[index] = value[:128]
        else:
            out[...] = value[:128].T
        if index == 0:
            vectors[...] = value[128:136, :128] + value[136:, :128]


def final_turned_kernel(own, *refs):
    value = own[...].astype(F32)
    for piece in refs[:3]:
        value = value + piece[...].astype(F32)
    refs[3][...] = value.T


def widen_kernel(total, out):
    columns = out.shape[2]
    for index in range(out.shape[0]):
        out[index] = total[:, index * columns : (index + 1) * columns].astype(F32)


def weight_grad_kernel(lefts, rights, first_steps, by_halves, parted, meta, order, *refs, rider=0):
    count = sum(lefts)
    left = refs[:count]
    right = refs[count : count + sum(rights)]
    riders = refs[count + sum(rights) : count + sum(rights) + rider]
    outs = refs[count + sum(rights) + rider : -3]
    rows, result, vectors = refs[-3:]
    slot = SLOT if rider else 128
    step = pl.program_id(0)

    def gather(pieces):
        start = 0
        for piece in pieces:
            size = piece.shape[-2]
            rows[start : start + size] = piece[0] if len(piece.shape) == 3 else piece[...]
            start += size

    def multiply(pieces):
        product = t_mm(rows[...], jnp.concatenate(pieces, axis=0)).astype(BF16)
        if not parted:
            outs[0][...] = product
            return
        result[...] = product
        slices = product.shape[0] // 128
        for spot in range(slices):
            out = outs[spot // (slices // 2)]
            start = spot % (slices // 2) * slot
            from_row = pl.multiple_of(order[spot] * 128, 128)
            out[start : start + 128] = result[pl.ds(from_row, 128)]
            if rider:
                value = vectors[:, pl.ds(from_row, 128)]
                high = value.astype(BF16).astype(F32)
                both = jnp.concatenate([high, value - high], axis=0)
                both = jnp.concatenate([both, jnp.zeros_like(both)], axis=1)
                out[start + 128 : start + slot] = both.astype(BF16)

    def flat(piece):
        return piece[0] if len(piece.shape) == 3 else piece[...]

    def split(piece):
        halves = []
        for part in (meta[0], 1 - meta[0]):
            for clip in range(piece.shape[0] // CLIP):
                halves.append(piece[pl.ds(pl.multiple_of(clip * CLIP + part * HALF, HALF), HALF)])
        return halves

    @pl.when(step == 0)
    def _():
        gather(left[: lefts[0]])
        if rider:
            third = rider // 3
            for place, source, size in ((0, 0, 2), (2, 1, 3), (5, 2, 1)):
                value = sum(ref[:size] for ref in riders[source * third : (source + 1) * third])
                if source == 1:
                    value = jnp.where(meta[meta.shape[0] - 1] > 0, value, 0.0)
                vectors[place : place + size] = value
            vectors[6:] = jnp.zeros((2, vectors.shape[1]), F32)

    if first_steps is None:
        multiply([flat(piece) for piece in right])
        return

    @pl.when(step == first_steps)
    def _():
        gather(left[lefts[0] :])

    @pl.when(step < first_steps)
    def _():
        multiply([flat(piece) for piece in right[: rights[0]]])

    @pl.when(step >= first_steps)
    def _():
        if by_halves:
            multiply([half for piece in right[rights[0] :] for half in split(piece)])
        else:
            multiply([flat(piece) for piece in right[rights[0] :]])


def shape(rows, columns, dtype=BF16):
    return jax.ShapeDtypeStruct((rows, columns), dtype)


def stored(*dims):
    return pltpu.HBM(dims, BF16)


def whole(*dims):
    return pl.BlockSpec(dims, lambda i, *_: (0,) * len(dims), pipeline_mode=pl.Buffered(1))


def total(*dims):
    return pl.BlockSpec(dims, lambda i, *_: (0,) * len(dims))


def smem():
    return pl.BlockSpec(memory_space=pltpu.SMEM)


def call(
    body, limit, inputs, in_specs, out_specs, out_shape, grid, scratch, us, after=(), prefetch=0,
    aliases={}, through=(),
):
    count = len(inputs)
    extra = len(after)
    through = list(through)
    outs = len(out_shape)
    aliases = dict(aliases)

    def kernel(*refs):
        results = refs[count + len(through) + extra :]
        body(*refs[:count], *results[:outs], *results[outs + len(through) :])

    out_specs, out_shape = list(out_specs), list(out_shape)
    in_specs = list(in_specs)
    for index, array in enumerate(through):
        aliases[count + index] = len(out_shape)
        out_specs.append(pl.BlockSpec(memory_space=pl.ANY))
        out_shape.append(jax.ShapeDtypeStruct(array.shape, array.dtype))
    return pl.pallas_call(
        kernel,
        grid_spec=pltpu.PrefetchScalarGridSpec(
            num_scalar_prefetch=prefetch,
            grid=grid,
            in_specs=in_specs + [pl.BlockSpec(memory_space=pl.ANY)] * (len(through) + extra),
            out_specs=out_specs,
            scratch_shapes=scratch,
        ),
        out_shape=out_shape,
        name=getattr(body, "func", body).__name__[:-7],
        compiler_params=pltpu.CompilerParams(vmem_limit_bytes=limit * MIB),
        cost_estimate=pl.CostEstimate(
            flops=int(us * 1.0e9) + 1, bytes_accessed=128, transcendentals=0
        ),
        input_output_aliases=aliases,
    )(*inputs, *through, *after)


def weight_grad(run, meta, order, limit, first, second, block, parted=True, rider=None):
    depth = first[0][0][0].shape[-1]
    specs, arrays, lefts, rights, steps = [], [], [], [], []
    products = [first] if second is None else [first, second]
    for left, _, _ in products:
        lefts.append(len(left))
        for array, group in left:
            arrays.append(array)
            if group is None:
                specs.append(whole(array.shape[0], depth))
            else:
                specs.append(
                    pl.BlockSpec(
                        (1, *array.shape[1:]), lambda i, group=group: (group, 0, 0),
                        pipeline_mode=pl.Buffered(1),
                    )
                )
    start = 0
    for _, right, groups in products:
        rights.append(len(right))
        count = right[0].shape[-1] // block
        total_steps = count * (1 if groups is None else len(groups))

        def at(i, start=start, total_steps=total_steps):
            return jnp.clip(i - start, 0, total_steps - 1)

        for array in right:
            arrays.append(array)
            rows = array.shape[-2]
            if groups is None:
                specs.append(pl.BlockSpec((rows, block), lambda i, at=at: (0, at(i))))
            else:
                specs.append(
                    pl.BlockSpec(
                        (1, rows, block),
                        lambda i, at=at, groups=groups, count=count: (
                            groups[0] + at(i) // count, 0, at(i) % count
                        ),
                    )
                )
        steps.append(total_steps)
        start += total_steps
    height = depth // 2
    if rider is not None:
        arrays += rider
        specs += [whole(*array.shape) for array in rider]
        height = depth // 256 * SLOT
    rows = sum(array.shape[-2] for array, _ in first[0])
    out = pl.BlockSpec((height, block), lambda i: (0, i))
    return run(
        functools.partial(
            weight_grad_kernel, lefts, rights, None if second is None else steps[0],
            second is not None and second[2] is None, parted, rider=0 if rider is None else len(rider),
        ),
        limit,
        [meta, order, *arrays],
        [smem(), smem()] + specs,
        [out] * 2 if parted else [pl.BlockSpec((depth, block), lambda i: (0, i))],
        [shape(height, start * block)] * 2 if parted else [shape(depth, start * block)],
        (start,),
        [
            pltpu.VMEM((rows, depth), BF16), pltpu.VMEM((depth, block), BF16),
            pltpu.VMEM((8, depth), F32),
        ], 20.0,
    )


def build(dp_size, chunks_of):
    cos_np, sin_np = tables()

    def per_device(
        inputs, cotangent, lengths, first_gain, first_bias, qkv_weight, out_weight, first_scale,
        second_gain, second_bias, in_weight, down_weight, second_scale,
    ):
        chunks = chunks_of(lengths.shape[0])
        depth = inputs.shape[1]
        width = out_weight.shape[0]
        units = down_weight.shape[0]
        place = lax.axis_index("tensor")
        spot = lax.axis_index("dp")
        core = place % 2
        once = (place < 2).astype(jnp.int32)
        meta = jnp.concatenate([core.reshape(1).astype(jnp.int32), lengths, once.reshape(1)])
        natural = jnp.arange(depth // 128, dtype=jnp.int32)
        if dp_size == 8:
            y, z = spot % 2, spot // 2
            order = jnp.stack(
                [2 * (z ^ hop) + y for hop in range(4)] + [2 * (z ^ hop) + 1 - y for hop in range(4)]
            ).astype(jnp.int32)
        else:
            order = natural
        cos_t = jnp.asarray(cos_np)
        sin_t = jnp.asarray(sin_np)
        row = lambda v: v.reshape(1, depth)
        first_gain, first_bias, first_scale = row(first_gain), row(first_bias), row(first_scale)
        second_gain, second_bias, second_scale = row(second_gain), row(second_bias), row(second_scale)

        chain, held = [], []

        def run(*arguments, **named):
            results = call(
                *arguments, after=tuple(chain), through=[at[key] for at, key in held], **named
            )
            chain[:] = [results[0]]
            results = list(results)
            for at, key in reversed(held):
                at[key] = results.pop()
            held.clear()
            return results

        def swap(values, bit):
            return lax.ppermute(values, "tensor", [(i, i ^ bit) for i in range(4)])

        out_other, in_other, down_other, qkv_other = (
            swap(weight, 1) for weight in (out_weight, in_weight, down_weight, qkv_weight)
        )
        half_rows = pl.BlockSpec((HALF, depth), lambda i, *m: (i, 0))
        half_head = pl.BlockSpec((HALF, width), lambda i, *m: (i, 0))
        own_head = pl.BlockSpec((HALF, width), lambda i, m: (2 * i + m[0], 0))
        clip_head = pl.BlockSpec((CLIP, width), lambda i, *m: (i, 0))

        def own_rows(first):
            return pl.BlockSpec((HALF, depth), lambda i, m: (2 * (first + i) + m[0], 0))

        def attend(chunk):
            first, count = chunk[0], len(chunk)
            pad = pltpu.VMEM((CLIP + 2 * TILE, width), BF16)
            return run(
                functools.partial(attend_kernel, first),
                63,
                [meta, inputs, first_gain, first_bias, qkv_weight, cos_t, sin_t],
                [
                    smem(), pl.BlockSpec((HALF, depth), lambda i: (2 * first + i, 0)), whole(1, depth),
                    whole(1, depth), whole(3, depth, width), whole(CLIP, 128), whole(CLIP, 128),
                ],
                [
                    half_rows, half_head, half_head, half_head,
                    pl.BlockSpec((CLIP, width), lambda i: (i // 2, 0)),
                    pl.BlockSpec((HALF, width), lambda i: (i // 2, 0)),
                ],
                [stored(count * CLIP, depth)] + [stored(count * CLIP, width)] * 4
                + [shape(count * HALF, width)],
                (2 * count,),
                [
                    pltpu.VMEM((CLIP, width), BF16), pad, pad, pltpu.VMEM((1, width), F32),
                    pltpu.VMEM((width // HEAD * TILE, SPAN), F32),
                ], 0.0 * count,
            )

        def project(chunk, heads, arrived):
            return run(
                project_kernel, 63,
                [meta, heads, arrived, out_weight, out_other],
                [own_head, half_head, whole(width, depth), whole(width, depth)],
                [half_rows], [shape(len(chunk) * HALF, depth)], (len(chunk),), [], 0.0 * len(chunk), prefetch=1,
            )[0]

        def feed(chunk, own, other):
            first, count = chunk[0], len(chunk)
            block = 512
            steps = units // block
            rows = count * HALF
            mine = lambda i: jnp.minimum(i, steps - 1)
            theirs = lambda i: jnp.maximum(i - steps, 0)
            local = [
                pl.BlockSpec(
                    (HALF, depth), lambda i, m, c=c: (2 * c + m[0], 0), pipeline_mode=pl.Buffered(1)
                )
                for c in chunk
            ]
            hidden = jax.ShapeDtypeStruct((5, rows, units), BF16)
            return run(
                functools.partial(feed_kernel, first, count),
                63,
                [meta, own, other, first_scale, second_gain, second_bias, second_scale]
                + [inputs] * count + [cotangent] * count
                + [in_weight, in_other, down_weight, down_other],
                [whole(rows, depth)] * 2 + [whole(1, depth)] * 4 + local + local
                + [
                    pl.BlockSpec(memory_space=pl.ANY) for _ in range(4)
                ],
                [
                    pl.BlockSpec((3, rows, block), lambda i, m: (0, 0, mine(i))),
                    pl.BlockSpec((5, rows, block), lambda i, m: (0, 0, theirs(i))),
                    whole(2, rows, depth), whole(rows, depth), whole(rows, depth), total(8, depth),
                ],
                [
                    stored(3, rows, units), hidden, jax.ShapeDtypeStruct((2, rows, depth), BF16),
                    shape(rows, depth), shape(rows, depth), shape(8, depth, F32),
                ],
                (2 * steps,),
                [pltpu.VMEM((rows, depth), F32)] * 2
                + [
                    pltpu.VMEM((2, 2, depth, block), BF16), pltpu.VMEM((2, block, depth), BF16),
                    pltpu.SemaphoreType.DMA((2, 2)),
                ], 15.0 * count,
                prefetch=1,
            )

        def middle_back(chunk, own, other, g_own, g_other):
            first, count = chunk[0], len(chunk)
            rows = count * HALF
            return run(
                functools.partial(middle_back_kernel, first),
                63,
                [
                    meta, own, other, g_own, g_other, inputs, cotangent, first_scale, second_gain,
                    out_weight, out_other,
                ],
                [half_rows] * 4 + [own_rows(first)] * 2 + [whole(1, depth)] * 2
                + [whole(width, depth)] * 2,
                [
                    half_rows, half_rows, half_head,
                    pl.BlockSpec((HALF, depth + width), lambda i, m: (i, 0)), total(8, depth),
                ],
                [
                    shape(rows, depth, F32), shape(rows, depth), shape(rows, width),
                    shape(rows, depth + width), shape(8, depth, F32),
                ],
                (count,), [], 200.0 if first == 0 else 10.0, prefetch=1,
            )

        def attend_back(chunk, own, other, q, k, v):
            first, count = chunk[0], len(chunk)
            pad = (CLIP + 2 * TILE, width)
            return run(
                functools.partial(attend_back_kernel, first),
                63,
                [meta, own, other, q, k, v, cos_t, sin_t],
                [
                    smem(), half_head,
                    pl.BlockSpec((HALF, width), lambda i: (i, depth // width)), clip_head, clip_head, clip_head,
                    whole(CLIP, 128), whole(CLIP, 128),
                ],
                [
                    pl.BlockSpec((CLIP, 3 * width), lambda i: (i, 0)),
                    pl.BlockSpec((HALF, 3 * width), lambda i: (i, 0)),
                ],
                [stored(count * CLIP, 3 * width), shape(count * HALF, 3 * width)],
                (count,),
                [
                    pltpu.VMEM(pad, BF16), pltpu.VMEM(pad, BF16), pltpu.VMEM(pad, F32),
                    pltpu.VMEM(pad, F32), pltpu.VMEM((CLIP, width), BF16),
                    pltpu.VMEM((CLIP, width), F32), pltpu.VMEM((width // HEAD * TILE, SPAN), F32),
                ], 16.0 * count,
            )

        def first_term(chunk, grads, arrived):
            first, count = chunk[0], len(chunk)
            return run(
                term_kernel, 63,
                [meta, grads, arrived, inputs, qkv_weight, qkv_other],
                [
                    pl.BlockSpec((HALF, 3 * width), lambda i, m: (2 * i + m[0], 0)),
                    pl.BlockSpec((HALF, 3 * width), lambda i, m: (i, 0)), own_rows(first),
                    whole(3, depth, width), whole(3, depth, width),
                ],
                [half_rows, total(8, depth)],
                [shape(count * HALF, depth), shape(8, depth, F32)],
                (count,), [], 16.0 * count, prefetch=1,
            )

        def finish(chunk, local, shared):
            first, count = chunk[0], len(chunk)
            return run(
                functools.partial(finish_kernel, first),
                63,
                [meta, *local, inputs, *shared],
                [half_rows] * len(local) + [own_rows(first)] + [whole(1, depth)] * len(shared),
                [pl.BlockSpec((2, HALF, depth), lambda i, m: (0, i, 0))],
                [jax.ShapeDtypeStruct((2, count * HALF, depth), BF16)], (count,), [],
                20.0, prefetch=1,
            )[0]

        def put(chunk, own, other, bases):
            first, count = chunk[0], len(chunk)
            part = pl.BlockSpec((2, HALF, depth), lambda i: (0, i, 0))
            return run(
                place_kernel,
                63,
                [meta, own, other, *bases],
                [smem(), part, part] + [pl.BlockSpec(memory_space=pl.ANY)] * len(bases),
                [pl.BlockSpec((CLIP, depth), lambda i: (first + i, 0))] * 2,
                [shape(inputs.shape[0], depth)] * 2,
                (count,), [], 16.0, aliases={3: 0, 4: 1} if bases else {},
            )

        def scatter_y(keep, send, body=sum_kernel):
            if dp_size != 8:
                whole_grad = jnp.concatenate([keep, send], axis=0)
                result = lax.psum_scatter(whole_grad, "dp", scatter_dimension=0, tiled=True)
                return lambda: result
            arrived = lax.ppermute(send, "dp", [(i, i ^ 1) for i in range(8)])
            rows, columns = keep.shape
            block = columns // (2 if columns % 512 == 0 else 1)
            part = pl.BlockSpec((rows, block), lambda i: (0, i))
            out = pl.BlockSpec((rows // 4, block), lambda i: (0, i))
            return lambda: run(
                body, 63, [keep, arrived], [part, part], [out] * 4,
                [shape(rows // 4, columns)] * 4, (columns // block,), [], 16.0,
            )

        def send_z(slices):
            return slices[:1] + [
                lax.ppermute(slices[hop], "dp", [(i, i ^ (2 * hop)) for i in range(8)])
                for hop in (1, 2, 3)
            ]

        def final(pieces):
            if dp_size != 8:
                value = pieces.astype(F32)
                qkv = jnp.stack([value[:, i * width : (i + 1) * width] for i in range(3)])
                return qkv, value[:, 3 * width :].T, None
            return run(
                final_kernel, 63, pieces, [whole(SLOT, 4 * width)] * 4,
                [total(3, 128, width), total(width, 128), total(8, 128)],
                [
                    jax.ShapeDtypeStruct((3, 128, width), F32), shape(width, 128, F32),
                    shape(8, 128, F32),
                ],
                (1,), [], 16.0,
            )

        def widen(value):
            rows = value.shape[0]
            return run(
                widen_kernel, 63, [value], [whole(rows, 2 * units)], [total(2, rows, units)],
                [jax.ShapeDtypeStruct((2, rows, units), F32)], (1,), [], 16.0,
            )[0]

        def final_turned(pieces):
            if dp_size != 8:
                return (pieces.astype(F32).T,)
            return run(
                final_turned_kernel, 63, pieces, [whole(128, units)] * 4, [total(units, 128)],
                [shape(units, 128, F32)], (1,), [], 16.0,
            )

        state = [dict() for _ in chunks]
        parts = list(zip(chunks, state))

        def ending(chunk, at):
            own = finish(
                chunk,
                [
                    at["own"], at["other"], at["ff"], at["ff_other"], at["g1"], at["g1_other"],
                    at["grad_one"],
                ],
                [first_scale, second_scale, first_gain],
            )
            other = swap(own, 1)
            return lambda bases: put(chunk, own, other, bases)

        def forward(chunk, at):
            at["normed"], at["q"], at["k"], at["v"], at["heads"], send = attend(chunk)
            at["heads_other"] = swap(send, 1)

        def projected(chunk, at):
            at["own"] = project(chunk, at["heads"], at["heads_other"])
            at["other"] = swap(at["own"], 2)

        def fed(chunk, at):
            at["kept"], send, at["rows"], at["gn"], at["ff"], at["feed_sums"] = feed(
                chunk, at["own"], at["other"]
            )
            at["gn_other"] = swap(at["gn"], 2)
            at["arrived"] = swap(send, 1)

        def middle(chunk, at):
            at["grad_one"], at["ga"], at["gh"], send, at["mid_sums"] = middle_back(
                chunk, at["own"], at["other"], at["gn"], at["gn_other"]
            )
            at["back_other"] = swap(send, 1)

        def back(chunk, at):
            at["dqkv"], send = attend_back(
                chunk, at["gh"], at["back_other"], at["q"], at["k"], at["v"]
            )
            at["dqkv_other"] = swap(send, 1)

        def term(chunk, at):
            at["g1"], at["term_sums"] = first_term(chunk, at["dqkv"], at["dqkv_other"])
            at["g1_other"] = swap(at["g1"], 2)

        def vectors():
            alike = sum(at["mid_sums"] for at in state)[0:3]
            backward = sum(at["term_sums"] for at in state)[0:2]
            forward = sum(at["feed_sums"] for at in state)[0:1]
            alike = jnp.where(place < 2, alike, 0.0)
            return jnp.concatenate([backward, alike, forward, jnp.zeros((2, depth), F32)], axis=0)

        def send_forward(at):
            at["ff_other"] = swap(at["ff"], 2)

        results = []
        forward(*parts[0])
        projected(*parts[0])
        forward(*parts[1])
        chain.extend([in_other, down_other, qkv_other])
        projected(*parts[1])
        fed(*parts[0])
        fed(*parts[1])
        n_pieces = [piece for at in state for piece in ((at["rows"], 0), (at["arrived"], 3))]
        gf_pieces = [piece for at in state for piece in ((at["rows"], 1), (at["arrived"], 4))]
        right = [at[key] for at in state for key in ("kept", "arrived")]
        middle(*parts[0])
        held.append((state[0], "ff"))
        (grads_in,) = weight_grad(
            run, meta, natural, 63, (n_pieces, right, (0, 1)), None, 512, False
        )
        in_sum = lax.psum_scatter(grads_in, "dp", scatter_dimension=0, tiled=True)
        send_forward(state[0])
        back(*parts[0])
        turned_sum = scatter_y(
            *weight_grad(run, meta, order, 63, (gf_pieces, right, (2,)), None, 512)
        )
        middle(*parts[1])
        held.append((state[1], "ff"))
        term(*parts[0])
        send_forward(state[1])
        back(*parts[1])
        place_0 = ending(*parts[0])
        term(*parts[1])
        turned_sum = turned_sum()
        if dp_size == 8:
            turned_sum = send_z(turned_sum)
        riders = [at[key] for key in ("term_sums", "mid_sums", "feed_sums") for at in state]
        qkv_sum = scatter_y(
            *weight_grad(
                run, meta, order, 63,
                ([(at["normed"], None) for at in state], [at["dqkv"] for at in state], None),
                (
                    [(at[key], None) for at in state for key in ("ga", "back_other")],
                    [at["heads"] for at in state], None,
                ),
                256, rider=riders if dp_size == 8 else None,
            ),
            sum_rider_kernel,
        )
        results = place_0(results)
        place_1 = ending(*parts[1])
        qkv_sum = qkv_sum()
        if dp_size == 8:
            qkv_sum = send_z(qkv_sum)
        (down_sum,) = final_turned(turned_sum)
        in_sum = widen(in_sum)
        results = place_1(results)
        qkv_sum, out_sum, mine = final(qkv_sum)

        if dp_size != 8:
            stacked = vectors()
            bit = 1
            while bit < dp_size:
                stacked = stacked + lax.ppermute(
                    stacked, "dp", [(i, i ^ bit) for i in range(dp_size)]
                )
                bit *= 2
            share = depth // dp_size
            mine = lax.dynamic_slice_in_dim(stacked, spot * share, share, 1)
        mine = mine + sum(swap(mine, bit) for bit in (1, 2, 3))

        return (
            *results,
            mine[0],
            mine[1],
            qkv_sum,
            out_sum,
            mine[2],
            mine[3],
            mine[4],
            in_sum,
            down_sum,
            mine[5],
        )

    return per_device


def in_chunks(clips):
    return [list(range(1)), list(range(1, clips))]


def solution(mesh):
    placed = (
        P("dp", None), P("dp", None), P("dp"), P(), P(), P(None, None, "tensor"),
        P("tensor", None), P(), P(), P(), P(None, None, "tensor"), P("tensor", None), P(),
    )
    return jax.shard_map(
        build(mesh.shape["dp"], in_chunks),
        mesh=mesh,
        in_specs=placed,
        out_specs=(
            P("dp", None), P("dp", None), P("dp"), P("dp"), P(None, "dp", "tensor"),
            P("tensor", "dp"), P("dp"), P("dp"), P("dp"), P(None, "dp", "tensor"),
            P("tensor", "dp"), P("dp"),
        ),
        check_vma=False,
    )
```
